32 devices in a mesh: rep: 8 (over y, x, core), tp: 4 (over z).
Axes of the slice: x: 2, y: 2, z: 4, core: 2. Of those that a mesh axis runs over, the one named last changes fastest.
Arguments:
- hidden_in: bfloat16 [768, 8192], P('rep', 'tp'), may hold values from -6 to 6
- queries: bfloat16 [768, 8192], P('rep', 'tp'), may hold values from -20 to 20
- cache_keys: bfloat16 [768, 128, 1024], P('rep', None, 'tp'), may hold values from -6 to 6
- cached_value_rows: bfloat16 [768, 128, 1024], P('rep', None, 'tp'), may hold values from -6 to 6
- cache_lengths: int32 [768], P('rep'), may hold values from 1 to 128, 24576 in all
- base_key_matrix: bfloat16 [8192, 1024], P(None, 'tp'), may hold values from -0.0625 to 0.0625
- base_value_matrix: bfloat16 [8192, 1024], P(None, 'tp'), may hold values from -0.0625 to 0.0625
- shrink_weights: bfloat16 [32, 8192, 128], P('rep', 'tp'), may hold values from -0.0625 to 0.0625
- pooled_up_weights: bfloat16 [32, 2, 64, 1024], P('rep', None, None, 'tp'), may hold values from -0.75 to 0.75
- block_owner: int32 [192, 1], P('rep'), may hold values from 0 to 7; in each aligned block of 24 rows (0 to 23, 24 to 47, ...) at most 6 rows name the same one
- block_slot: int32 [192], P('rep'), may hold values from 0 to 3
Outputs:
- new_keys: bfloat16 [768, 1024], P('rep', 'tp')
- new_values: bfloat16 [768, 1024], P('rep', 'tp')
- context: bfloat16 [768, 8192], P('rep', 'tp')
The draws below stay inside these ranges and needn't reach their ends.
Inputs may be any that keep to these rules, and one draw needn't show every extreme that they name: `block_owner`: among the 24 blocks of one replica group at most 6 name the same owner, and some group in every draw has 6 blocks with one owner.
All inputs are finite; a program needn't handle non-finite values. No bound on the sum of `cache_lengths` on one device may be relied on, other than what follows from the above.
Results may differ from the reference program's by a relative error of at most 0.0055.
Values may be sent and summed in bfloat16 or wider, within the bound.
No kernel may reach another device: no remote copies, remote signals or barrier semaphores. Data moves between devices by JAX's collectives and lax.ppermute only.
A program may use at most 128 MiB of HBM per device.

```python
import math
import jax
import jax.numpy as jnp
import numpy as np
from jax import lax

MODEL_WIDTH = 8192
QUERY_HEAD_COUNT = 64
KEY_VALUE_HEADS = 8
HEAD_SIZE = 128
ADAPTER_RANK = 64
ADP_DEV = 4
ADAPTER_POOL = 32
ROWS_DEV = 96
SEQUENCE_COUNT = 768
BLK = 4
BLOCKS = 24
CAP = 6
CONTEXT_LENGTH = 128
N_REP = 8


def draw_queries(key, part):
    drawn_result = jnp.clip(jax.random.normal(jax.random.fold_in(key, 21), (SEQUENCE_COUNT, QUERY_HEAD_COUNT * HEAD_SIZE), jnp.float32), -6.0, 6.0)
    return drawn_result.astype(jnp.bfloat16)


def draw_cache_keys(key, part):
    drawn_result = jnp.clip(jax.random.normal(jax.random.fold_in(key, 31), (SEQUENCE_COUNT, CONTEXT_LENGTH, KEY_VALUE_HEADS * HEAD_SIZE), jnp.float32), -6.0, 6.0)
    return drawn_result.astype(jnp.bfloat16)


def place_ends(drawn, key, smallest, largest):
    longest = drawn.shape.index(max(drawn.shape))
    spots = []
    for shift in (0, 1):
        where = [jax.random.randint(jax.random.fold_in(key, axis), (), 0, length) for axis, length in enumerate(drawn.shape)]
        where[longest] = (where[longest] + shift) % drawn.shape[longest]
        spots.append(tuple(where))
    return drawn.at[spots[0]].set(smallest).at[spots[1]].set(largest)


def level_of(rng, shape, cuts, low, high):
    level = 1.0
    for dim, parts in cuts:
        draws = jax.random.uniform(jax.random.fold_in(jax.random.fold_in(rng, 6), dim), (parts,), jnp.float32, low / len(cuts), high / len(cuts))
        level = level * jnp.repeat(jnp.exp(draws), shape[dim] // parts).reshape((-1,) + (1,) * (len(shape) - 1 - dim))
    return level


def profile(number_of, total, reach, slope):
    portions = [(1 << 20) // math.isqrt(standing ** slope) + 1 for standing in range(2, number_of + 1)]
    spare, counts = total - reach - (number_of - 1), [1] * (number_of - 1)
    while spare > 0:
        candidates = [i for i in range(number_of - 1) if counts[i] < reach]
        mass, budget = sum([portions[i] for i in candidates]), spare
        for i in candidates:
            more = min(reach - counts[i], max(1, budget * portions[i] // mass), spare)
            counts[i] = counts[i] + more
            spare = spare - more
    return np.array([reach] + counts)


def uneven(stream_key, number_of, total, reach, slope):
    if number_of == 2:
        one = jax.random.randint(stream_key, (), max(1, total - reach), min(reach, total - 1) + 1)
        return jnp.stack([one, total - one])
    sizes = jnp.asarray(profile(number_of, total, reach, slope), jnp.int32)
    twos = (number_of - 1) // 2
    donor, taker = sizes[1:1 + 2 * twos:2], sizes[2:2 + 2 * twos:2]
    margin = jnp.minimum(donor - 1, reach - taker)
    passed = jax.random.randint(jax.random.fold_in(stream_key, 1), (twos,), 0, 1 << 20) % (margin + 1)
    sizes = sizes.at[1:1 + 2 * twos:2].set(donor - passed).at[2:2 + 2 * twos:2].set(taker + passed)
    return sizes[jax.random.permutation(jax.random.fold_in(stream_key, 2), number_of)]


def deal_out(rng, own, number, rows, count, top, most, skew):
    sequence = jax.random.permutation(rng, count)
    packed, ordinary = shares(count, rows * top, most, skew, True), shares(count, rows * top, most, skew, False)
    places = jnp.arange(count)

    def named(sizes, turn):
        used = int((sizes > 0).sum())
        fixed = max(1, used // 4)
        shifted = fixed + (places - fixed + turn * (used - fixed)) % max(1, count - fixed)
        return jnp.zeros((count,), jnp.int32).at[sequence[jnp.where(places < fixed, places, shifted)]].set(jnp.asarray(sizes, jnp.int32))

    sizes = jnp.where(number % 4 == 0, named(packed, number // 4), named(ordinary, number - number // 4 - 1))
    mixed = jax.random.permutation(jax.random.fold_in(own, 3), count)
    donor, sink = mixed[0:count // 2 * 2:2], mixed[1:count // 2 * 2:2]
    slack = jnp.minimum(sizes[donor] - 1, most - sizes[sink]) // 2
    slack = jnp.where((donor == sequence[0]) | (sink == sequence[0]) | (sizes[sink] == 0), 0, jnp.maximum(slack, 0))
    shifted = jax.random.randint(jax.random.fold_in(own, 4), (count // 2,), 0, 1 << 20) % (slack + 1)
    sizes = sizes.at[donor].add(-shifted).at[sink].add(shifted)
    labels = jnp.searchsorted(jnp.cumsum(sizes), jnp.arange(rows * top), side="right").astype(jnp.int32)
    listing = labels.reshape(top, rows).T
    listing = listing[jax.random.permutation(jax.random.fold_in(own, 1), rows)]
    turn = jax.random.randint(jax.random.fold_in(own, 2), (rows, 1), 0, top)
    return jnp.take_along_axis(listing, (jnp.arange(top)[None, :] + turn) % top, axis=1)


def shares(count, total, most, slope, full):
    portions = [(1 << 20) // math.isqrt(standing ** slope) + 1 for standing in range(1, count + 1)]
    largest = most if full else min(most, max(-(-total // count), total * portions[0] // sum(portions)))
    least = 1 if total - largest >= count - 1 else 0
    holding, spare = [largest] + [least] * (count - 1), total - largest - least * (count - 1)
    while spare > 0:
        candidates = [i for i in range(1, count) if holding[i] < largest] or [i for i in range(1, count) if holding[i] < most]
        pool, left = sum([portions[i] for i in candidates]), spare
        for i in candidates:
            more = min(most - holding[i], max(1, left * portions[i] // pool), spare)
            holding[i] = holding[i] + more
            spare = spare - more
    return np.array(holding)


def normal_values(rng, dims, deviation, most, cuts=(), kind=jnp.bfloat16):
    entries = jax.random.normal(rng, dims, jnp.float32) * deviation
    if len(cuts) > 0:
        entries = level_of(rng, dims, cuts, -0.22, 0.18) * entries
    return jnp.clip(entries, min=-most, max=most).astype(kind)


def setup_inputs(seed: int = 0) -> dict:
    splits = jax.random.split(jax.random.key(seed), 12)
    hidden_in = normal_values(splits[0], (SEQUENCE_COUNT, MODEL_WIDTH), 1.0, 6.0, ((0, 8), (1, 4)))
    queries = draw_queries(jax.random.fold_in(splits[11], 71), 0)
    cache_keys = draw_cache_keys(jax.random.fold_in(splits[11], 71), 0)
    cached_value_rows = normal_values(splits[3], (SEQUENCE_COUNT, CONTEXT_LENGTH, KEY_VALUE_HEADS * HEAD_SIZE), 1.0, 6.0, ((0, 8), (2, 4)))
    cache_lengths = uneven(splits[4], SEQUENCE_COUNT, SEQUENCE_COUNT * CONTEXT_LENGTH // 4, CONTEXT_LENGTH, 2).astype(jnp.int32)
    base_key_matrix = normal_values(splits[5], (MODEL_WIDTH, KEY_VALUE_HEADS * HEAD_SIZE), MODEL_WIDTH ** -0.5, 0.0625, ((1, 4),))
    base_value_matrix = normal_values(splits[6], (MODEL_WIDTH, KEY_VALUE_HEADS * HEAD_SIZE), MODEL_WIDTH ** -0.5, 0.0625, ((1, 4),))
    shrink_weights = normal_values(splits[7], (ADAPTER_POOL, MODEL_WIDTH, 2 * ADAPTER_RANK), MODEL_WIDTH ** -0.5, 0.0625, ((0, 8), (1, 4)))
    pooled_up_weights = normal_values(splits[8], (ADAPTER_POOL, 2, ADAPTER_RANK, KEY_VALUE_HEADS * HEAD_SIZE), ADAPTER_RANK ** -0.5, 0.75, ((0, 8), (3, 4)))
    block_owner_keys = jax.random.split(jax.random.fold_in(splits[9], 1), (N_REP * BLOCKS) // BLOCKS)
    block_owner_turns = jax.random.permutation(jax.random.fold_in(splits[9], 3), (N_REP * BLOCKS) // BLOCKS)
    block_owner = jax.vmap(lambda own, number: deal_out(jax.random.fold_in(splits[9], 2), own, number, BLOCKS, N_REP, 1, CAP, 2))(block_owner_keys, block_owner_turns).reshape((N_REP * BLOCKS, 1))
    block_slot = place_ends(jax.random.randint(splits[10], (N_REP * BLOCKS,), 0, ADP_DEV), jax.random.fold_in(splits[10], 1), 0, ADP_DEV - 1).astype(jnp.int32)
    return dict(hidden_in=hidden_in, queries=queries, cache_keys=cache_keys, cached_value_rows=cached_value_rows, cache_lengths=cache_lengths, base_key_matrix=base_key_matrix, base_value_matrix=base_value_matrix, shrink_weights=shrink_weights, pooled_up_weights=pooled_up_weights, block_owner=block_owner, block_slot=block_slot)


adapter_scale = 0.5
masked_score = -1e30


def attend(group_queries, key_cache, value_cache, lengths, fresh_keys, fresh_values):
    rows_here = group_queries.shape[0]
    head_groups = key_cache.shape[2] // HEAD_SIZE
    group_size = group_queries.shape[1] // (head_groups * HEAD_SIZE)
    window = key_cache.shape[1]
    inverse_root = HEAD_SIZE ** -0.5
    query_heads = group_queries.reshape(rows_here, head_groups, group_size, HEAD_SIZE).astype(jnp.float32)
    key_heads = key_cache.reshape(rows_here, window, head_groups, HEAD_SIZE).astype(jnp.float32)
    value_heads = value_cache.reshape(rows_here, window, head_groups, HEAD_SIZE).astype(jnp.float32)
    scores = jnp.einsum('rkgd,rtkd->rkgt', query_heads, key_heads) * inverse_root
    own_score = jnp.einsum('rkgd,rkd->rkg', query_heads, fresh_keys.reshape(rows_here, head_groups, HEAD_SIZE).astype(jnp.float32)) * inverse_root
    visible = (jnp.arange(window, dtype=jnp.int32)[None, :] < lengths[:, None])[:, None, None, :]
    highest = jnp.maximum(jnp.max(jnp.where(visible, scores, masked_score), axis=-1), own_score)
    exp_terms = jnp.where(visible, jnp.exp(scores - highest[..., None]), 0.0)
    own_term = jnp.exp(own_score - highest)
    denominator = jnp.sum(exp_terms, axis=-1) + own_term
    weights = (exp_terms / denominator[..., None]).astype(jnp.bfloat16)
    own_weight = (own_term / denominator).astype(jnp.bfloat16)
    context = jnp.einsum('rkgt,rtkd->rkgd', weights.astype(jnp.float32), value_heads)
    context = context + own_weight.astype(jnp.float32)[..., None] * fresh_values.reshape(rows_here, head_groups, 1, HEAD_SIZE).astype(jnp.float32)
    return context.reshape(rows_here, -1).astype(jnp.bfloat16)


def reference(hidden_in, queries, cache_keys, cached_value_rows, cache_lengths, base_key_matrix, base_value_matrix, shrink_weights, pooled_up_weights, block_owner, block_slot):
    key_row_width = KEY_VALUE_HEADS * HEAD_SIZE

    def one_group(pieces):
        inputs, group_queries, group_keys, group_values, lengths, owners, slot_ids = pieces
        position = (owners[:, 0] * ADP_DEV + slot_ids).astype(jnp.int32)
        chosen_shrink = jnp.take(shrink_weights, position, axis=0).astype(jnp.float32)
        selected_expand = jnp.take(pooled_up_weights, position, axis=0).astype(jnp.float32)
        blocked = inputs.reshape(BLOCKS, BLK, MODEL_WIDTH).astype(jnp.float32)
        shrunk = jnp.einsum('bnd,bdr->bnr', blocked, chosen_shrink).astype(jnp.bfloat16)
        split_halves = shrunk.astype(jnp.float32).reshape(BLOCKS, BLK, 2, ADAPTER_RANK)
        per_row_delta = (adapter_scale * jnp.einsum('gfot,gotx->gfox', split_halves, selected_expand)).astype(jnp.bfloat16)
        per_row_delta = per_row_delta.reshape(ROWS_DEV, 2, key_row_width)
        base_keys = jnp.dot(inputs, base_key_matrix, preferred_element_type=jnp.float32)
        base_values = jnp.dot(inputs, base_value_matrix, preferred_element_type=jnp.float32)
        fresh_keys = (base_keys + per_row_delta[:, 0].astype(jnp.float32)).astype(jnp.bfloat16)
        fresh_values = (base_values + per_row_delta[:, 1].astype(jnp.float32)).astype(jnp.bfloat16)
        context = attend(group_queries, group_keys, group_values, lengths, fresh_keys, fresh_values)
        return fresh_keys, fresh_values, context

    pieces = (hidden_in.reshape(N_REP, ROWS_DEV, MODEL_WIDTH),
              queries.reshape(N_REP, ROWS_DEV, QUERY_HEAD_COUNT * HEAD_SIZE),
              cache_keys.reshape(N_REP, ROWS_DEV, CONTEXT_LENGTH, key_row_width),
              cached_value_rows.reshape(N_REP, ROWS_DEV, CONTEXT_LENGTH, key_row_width),
              cache_lengths.reshape(N_REP, ROWS_DEV),
              block_owner.reshape(N_REP, BLOCKS, 1),
              block_slot.reshape(N_REP, BLOCKS))
    fresh_keys, fresh_values, context = lax.map(one_group, pieces)
    return (fresh_keys.reshape(SEQUENCE_COUNT, key_row_width), fresh_values.reshape(SEQUENCE_COUNT, key_row_width), context.reshape(SEQUENCE_COUNT, QUERY_HEAD_COUNT * HEAD_SIZE))
```

```python
import functools

import jax
import jax.numpy as jnp
from jax import lax
from jax.experimental import pallas as pl
from jax.experimental.pallas import tpu as pltpu
from jax.sharding import PartitionSpec as P

HEAD_SIZE = 128
BLK = 4
LANES = 128
MIB = 1 << 20

adapter_scale = 0.5
masked_score = -1e30


def params(mib):
    return pltpu.CompilerParams(vmem_limit_bytes=mib * MIB)


def cost(flops, moved, exps=0):
    return pl.CostEstimate(flops=flops, bytes_accessed=moved, transcendentals=exps)


def iota(shape, dim):
    return lax.broadcasted_iota(jnp.int32, shape, dim)


def pack_kernel(capacity, owner_ref, slot_ref, hidden_ref, out_ref, pick_ref):
    blocks = owner_ref.shape[0]
    rows, width = hidden_ref.shape
    places = out_ref.shape[0]
    square = (blocks, blocks)
    down, across = iota(square, 0), iota(square, 1)
    owner_down = jnp.broadcast_to(owner_ref[...].astype(jnp.float32), square)
    slot_down = jnp.broadcast_to(slot_ref[...].astype(jnp.float32), square)
    owner_across = jnp.sum(jnp.where(down == across, owner_down, 0.0), axis=0, keepdims=True)
    slot_across = jnp.sum(jnp.where(down == across, slot_down, 0.0), axis=0, keepdims=True)
    same = (owner_down == owner_across) & (across < down)
    rank = jnp.sum(jnp.where(same, 1.0, 0.0), axis=1, keepdims=True)
    target = owner_ref[...].astype(jnp.float32) * capacity + rank
    spread = iota((blocks, rows), 0) == iota((blocks, rows), 1) // BLK
    row_target = jnp.sum(jnp.where(spread, jnp.broadcast_to(target, (blocks, rows)), 0.0), axis=0, keepdims=True)
    row_target = row_target.astype(jnp.int32) * BLK + iota((1, rows), 1) % BLK
    pick = jnp.where(iota((places, rows), 0) == row_target, 1.0, 0.0).astype(jnp.bfloat16)
    pick_ref[...] = pick
    gather = iota((rows, blocks), 1) == iota((rows, blocks), 0) // BLK
    row_slot = jnp.sum(jnp.where(gather, jnp.broadcast_to(slot_across, (rows, blocks)), 0.0), axis=1, keepdims=True)
    flags = jnp.where(iota((rows, LANES), 1) == row_slot.astype(jnp.int32), 1.0, 0.0).astype(jnp.bfloat16)
    out_ref[:, :width] = jnp.dot(pick, hidden_ref[...], preferred_element_type=jnp.float32).astype(jnp.bfloat16)
    out_ref[:, width:] = jnp.dot(pick, flags, preferred_element_type=jnp.float32).astype(jnp.bfloat16)


def pack(block_owner, block_slot, hidden, replicas, capacity):
    rows, width = hidden.shape
    places = replicas * capacity * BLK
    return pl.pallas_call(
        functools.partial(pack_kernel, capacity),
        name="pack_rows",
        out_shape=(
            jax.ShapeDtypeStruct((places, width + LANES), jnp.bfloat16),
            jax.ShapeDtypeStruct((places, rows), jnp.bfloat16),
        ),
        compiler_params=params(24),
        cost_estimate=cost(2 * places * rows * width, 2 * (places + rows) * width),
    )(block_owner, block_slot[:, None], hidden)


def shrink_kernel(rows_ref, shrink_ref, out_ref):
    pool, width, rank = shrink_ref.shape
    rows = rows_ref[:, :width]
    total = jnp.zeros(out_ref.shape, jnp.float32)
    for a in range(pool):
        part = jnp.dot(rows, shrink_ref[a], preferred_element_type=jnp.float32)
        total += part * rows_ref[:, width + a : width + a + 1].astype(jnp.float32)
    out_ref[...] = total.astype(out_ref.dtype)


def shrink(arrived, weights):
    places = arrived.shape[0]
    pool, width, rank = weights.shape
    return pl.pallas_call(
        shrink_kernel,
        name="shrink_rows",
        out_shape=jax.ShapeDtypeStruct((places, rank), jnp.bfloat16),
        compiler_params=params(24),
        cost_estimate=cost(2 * places * width * rank * pool, 2 * (places * width + weights.size)),
    )(arrived, weights)


def expand_kernel(count, *refs):
    parts, flag_ref, up_ref, out_ref = refs[:count], refs[count], refs[count + 1], refs[count + 2]
    pool, halves, rank, width = up_ref.shape
    total = parts[0][...].astype(jnp.float32)
    for part in parts[1:]:
        total += part[...].astype(jnp.float32)
    shrunk = total.astype(jnp.bfloat16)
    for half in range(halves):
        mine = shrunk[:, half * rank : (half + 1) * rank]
        wide = jnp.concatenate([mine * flag_ref[:, a : a + 1] for a in range(pool)], axis=1)
        table = up_ref[:, half].reshape(pool * rank, width)
        product = jnp.dot(wide, table, preferred_element_type=jnp.float32)
        out_ref[:, half * width : (half + 1) * width] = (adapter_scale * product).astype(jnp.bfloat16)


def expand(parts, arrived, up):
    places, rank2 = parts[0].shape
    pool, halves, rank, width = up.shape
    last = arrived.shape[1] // LANES - 1
    return pl.pallas_call(
        functools.partial(expand_kernel, len(parts)),
        name="expand_rows",
        grid=(1,),
        in_specs=[pl.BlockSpec((places, rank2), lambda i: (0, 0))] * len(parts)
        + [
            pl.BlockSpec((places, LANES), lambda i: (0, last)),
            pl.BlockSpec(up.shape, lambda i: (0, 0, 0, 0)),
        ],
        out_specs=pl.BlockSpec((places, halves * width), lambda i: (0, 0)),
        out_shape=jax.ShapeDtypeStruct((places, halves * width), jnp.bfloat16),
        compiler_params=params(16),
        cost_estimate=cost(2 * places * up.size, 2 * up.size + 2 * places * halves * width),
    )(*parts, arrived, up)


def cached_kernel(heads, length_ref, query_ref, key_ref, value_ref, mean_ref, lse_ref, wide_q, wide_o, wide_l):
    step = pl.program_id(0)
    rows, window, width = key_ref.shape
    groups = width // HEAD_SIZE
    each = heads // groups
    inverse_root = HEAD_SIZE ** (-0.5)

    @pl.when(step == 0)
    def _():
        wide_q[...] = jnp.zeros_like(wide_q)

    for h in range(heads):
        wide_q[h // each, pl.ds(h, rows, stride=heads), :] = query_ref[:, h * HEAD_SIZE : (h + 1) * HEAD_SIZE].astype(jnp.float32)
    lane = iota((heads, window), 1)
    for r in range(rows):
        here = pl.ds(r * heads, heads)
        query = jnp.concatenate([wide_q[k, here, :] for k in range(groups)], axis=1).astype(jnp.bfloat16)
        scores = lax.dot_general(query, key_ref[r], (((1,), (1,)), ((), ())), preferred_element_type=jnp.float32)
        scores = jnp.where(lane < length_ref[step * rows + r], scores * inverse_root, masked_score)
        highest = jnp.max(scores, axis=1, keepdims=True)
        terms = jnp.exp(scores - highest)
        total = jnp.sum(terms, axis=1, keepdims=True)
        mixed = jnp.dot(terms.astype(jnp.bfloat16), value_ref[r], preferred_element_type=jnp.float32)
        mixed = jnp.concatenate(
            [mixed[k * each : (k + 1) * each, k * HEAD_SIZE : (k + 1) * HEAD_SIZE] for k in range(groups)], axis=0
        )
        wide_o[here, :] = mixed / total
        wide_l[here, :] = jnp.broadcast_to(highest + jnp.log(total), (heads, LANES))
    place = iota((rows, LANES), 1)
    logs = jnp.zeros((rows, LANES), jnp.float32)
    for h in range(heads):
        mean_ref[:, h * HEAD_SIZE : (h + 1) * HEAD_SIZE] = wide_o[pl.ds(h, rows, stride=heads), :]
        logs = jnp.where(place == h, wide_l[pl.ds(h, rows, stride=heads), :], logs)
    lse_ref[...] = logs


def cached_attention(lengths, queries, keys, values):
    rows, window, width = keys.shape
    wide = queries.shape[1]
    heads = wide // HEAD_SIZE
    group = 16
    row_block = pl.BlockSpec((group, wide), lambda i, n: (i, 0))
    cache_block = pl.BlockSpec((group, window, width), lambda i, n: (i, 0, 0))
    return pl.pallas_call(
        functools.partial(cached_kernel, heads),
        name="cached_attention",
        grid_spec=pltpu.PrefetchScalarGridSpec(
            num_scalar_prefetch=1,
            grid=(rows // group,),
            in_specs=[row_block, cache_block, cache_block],
            out_specs=[row_block, pl.BlockSpec((group, LANES), lambda i, n: (i, 0))],
            scratch_shapes=[
                pltpu.VMEM((width // HEAD_SIZE, group * heads, HEAD_SIZE), jnp.float32),
                pltpu.VMEM((group * heads, HEAD_SIZE), jnp.float32),
                pltpu.VMEM((group * heads, LANES), jnp.float32),
            ],
        ),
        out_shape=(
            jax.ShapeDtypeStruct((rows, wide), jnp.float32),
            jax.ShapeDtypeStruct((rows, LANES), jnp.float32),
        ),
        compiler_params=params(24),
        cost_estimate=cost(4 * rows * heads * window * width, 4 * keys.size + 6 * rows * wide, rows * heads * window),
    )(lengths, queries, keys, values)


def base_kernel(count, index_ref, *refs):
    pieces, key_ref, value_ref, out_ref = refs[:count], refs[count], refs[count + 1], refs[count + 2]
    piece, step = pl.program_id(0), pl.program_id(1)
    depth, width = key_ref.shape

    @pl.when((piece == 0) & (step == 0))
    def _():
        out_ref[...] = jnp.zeros_like(out_ref)

    for p in range(count):

        @pl.when(piece == p)
        def _():
            rows = pieces[p][:, pl.ds(pl.multiple_of(step * depth, depth), depth)]
            out_ref[:, :width] += jnp.dot(rows, key_ref[...], preferred_element_type=jnp.float32)
            out_ref[:, width:] += jnp.dot(rows, value_ref[...], preferred_element_type=jnp.float32)


def base_products(pieces, index, key_matrix, value_matrix):
    rows, shard = pieces[0].shape
    width = key_matrix.shape[1]
    depth = min(1024, shard)
    steps = shard // depth
    weight = pl.BlockSpec((depth, width), lambda p, k, n: (n[p] * steps + k, 0))
    return pl.pallas_call(
        functools.partial(base_kernel, len(pieces)),
        name="base_products",
        grid_spec=pltpu.PrefetchScalarGridSpec(
            num_scalar_prefetch=1,
            grid=(len(pieces), steps),
            in_specs=[pl.BlockSpec((rows, shard), lambda p, k, n: (0, 0))] * len(pieces) + [weight, weight],
            out_specs=pl.BlockSpec((rows, 2 * width), lambda p, k, n: (0, 0)),
        ),
        out_shape=jax.ShapeDtypeStruct((rows, 2 * width), jnp.float32),
        compiler_params=params(24),
        cost_estimate=cost(4 * len(pieces) * rows * shard * width, len(pieces) * (4 * shard * width + 2 * rows * shard)),
    )(index, *pieces, key_matrix, value_matrix)


def finish_kernel(count, info_ref, *refs):
    late = refs[:count]
    key_ref, value_ref, base_ref, back_ref, pick_ref, query_ref, mean_ref, lse_ref = refs[count : count + 8]
    new_key_ref, new_value_ref, context_ref = refs[count + 8 :]
    rows, wide = query_ref.shape
    width = key_ref.shape[1]
    heads = wide // HEAD_SIZE
    each = heads // (width // HEAD_SIZE)
    inverse_root = HEAD_SIZE ** (-0.5)
    piece = late[0][...]
    for other in range(1, count):
        piece = jnp.where(info_ref[1] == other, late[other][...], piece)
    delta = lax.dot_general(pick_ref[...], back_ref[...], (((0,), (0,)), ((), ())), preferred_element_type=jnp.float32)
    base = base_ref[...] + delta
    keys = base[:, :width] + jnp.dot(piece, key_ref[...], preferred_element_type=jnp.float32)
    keys = keys.astype(jnp.bfloat16)
    new_key_ref[...] = keys
    values = base[:, width:] + jnp.dot(piece, value_ref[...], preferred_element_type=jnp.float32)
    values = values.astype(jnp.bfloat16)
    new_value_ref[...] = values
    keys, values = keys.astype(jnp.float32), values.astype(jnp.float32)
    place = iota((rows, LANES), 1)
    own = jnp.zeros((rows, LANES), jnp.float32)
    for h in range(heads):
        k = h // each
        query = query_ref[:, h * HEAD_SIZE : (h + 1) * HEAD_SIZE].astype(jnp.float32)
        score = jnp.sum(query * keys[:, k * HEAD_SIZE : (k + 1) * HEAD_SIZE], axis=1, keepdims=True)
        own = jnp.where(place == h, score * inverse_root, own)
    share = 1.0 / (1.0 + jnp.exp(lse_ref[...] - own))
    for h in range(heads):
        k = h // each
        mean = mean_ref[:, h * HEAD_SIZE : (h + 1) * HEAD_SIZE]
        mixed = mean + share[:, h : h + 1] * (values[:, k * HEAD_SIZE : (k + 1) * HEAD_SIZE] - mean)
        context_ref[:, h * HEAD_SIZE : (h + 1) * HEAD_SIZE] = mixed.astype(jnp.bfloat16)


def finish(late, info, key_matrix, value_matrix, base, back, pick, queries, mean, lse):
    rows, wide = queries.shape
    shard = late[0].shape[1]
    width = key_matrix.shape[1]

    def whole(array):
        return pl.BlockSpec(array.shape, lambda i, n: (0, 0))

    weight = pl.BlockSpec((shard, width), lambda i, n: (n[0], 0))
    rest = [base, back, pick, queries, mean, lse]
    outs = (
        jax.ShapeDtypeStruct((rows, width), jnp.bfloat16),
        jax.ShapeDtypeStruct((rows, width), jnp.bfloat16),
        jax.ShapeDtypeStruct((rows, wide), jnp.bfloat16),
    )
    return pl.pallas_call(
        functools.partial(finish_kernel, len(late)),
        name="finish_rows",
        grid_spec=pltpu.PrefetchScalarGridSpec(
            num_scalar_prefetch=1,
            grid=(1,),
            in_specs=[whole(a) for a in late] + [weight, weight] + [whole(a) for a in rest],
            out_specs=[whole(a) for a in outs],
        ),
        out_shape=outs,
        compiler_params=params(32),
        cost_estimate=cost(4 * rows * shard * width, 4 * shard * width + 10 * rows * wide),
    )(info, *late, key_matrix, value_matrix, *rest)


def swap(x, mask, size):
    return lax.ppermute(x, "tp", [(i, i ^ mask) for i in range(size)])


def turn(x, shift, size):
    return lax.ppermute(x, "tp", [(i, (i + shift) % size) for i in range(size)])


def others(x, size):
    return [turn(x, shift, size) for shift in range(1, size)]


def shards(
    hidden_in,
    queries,
    cache_keys,
    cached_value_rows,
    cache_lengths,
    base_key_matrix,
    base_value_matrix,
    shrink_weights,
    pooled_up_weights,
    block_owner,
    block_slot,
):
    rows_here, shard_width = hidden_in.shape
    replicas = lax.axis_size("rep")
    parts = lax.axis_size("tp")
    place = lax.axis_index("tp")
    blocks_here = rows_here // BLK
    capacity = max(2, (2 * blocks_here + replicas - 1) // replicas)
    width = base_key_matrix.shape[1]

    def all_to_all(x):
        kept = x.shape
        x = x.reshape(replicas, kept[0] // replicas, kept[1])
        return lax.all_to_all(x, "rep", split_axis=0, concat_axis=0, tiled=True).reshape(kept)

    outgoing, pick = pack(block_owner, block_slot, hidden_in, replicas, capacity)
    arrived = all_to_all(outgoing)

    if parts == 4:
        two = swap(hidden_in, 2, parts)
        one = swap(hidden_in, 1, parts)
        inner = lax.ppermute(hidden_in, "tp", [(1, 2), (2, 1)])
        outer = lax.ppermute(two, "tp", [(1, 0), (2, 3)])
        early, late = [hidden_in, one, two], [inner, outer]
        index = jnp.stack([place, place ^ 1, place ^ 2]).astype(jnp.int32)
        is_outer = ((place == 0) | (place == parts - 1)).astype(jnp.int32)
        info = jnp.stack([place ^ 3, is_outer]).astype(jnp.int32)
    else:
        pieces = [hidden_in] + others(hidden_in, parts)
        early, late = pieces[:-1], pieces[-1:]
        index = ((place + parts - jnp.arange(parts - 1, dtype=jnp.int32)) % parts).astype(jnp.int32)
        info = jnp.stack([(place + 1) % parts, place * 0]).astype(jnp.int32)

    mean, lse = cached_attention(cache_lengths, queries, cache_keys, cached_value_rows)
    partial_rows = shrink(arrived, shrink_weights)
    if parts == 4:
        sums = [partial_rows] + [swap(partial_rows, mask, parts) for mask in (1, 2, 3)]
    else:
        sums = [partial_rows] + others(partial_rows, parts)
    back = all_to_all(expand(sums, arrived, pooled_up_weights))
    base = base_products(early, index, base_key_matrix, base_value_matrix)
    return finish(late, info, base_key_matrix, base_value_matrix, base, back, pick, queries, mean, lse)


def solution(mesh):
    return jax.shard_map(
        shards,
        mesh=mesh,
        in_specs=(
            P("rep", "tp"),
            P("rep", "tp"),
            P("rep", None, "tp"),
            P("rep", None, "tp"),
            P("rep"),
            P(None, "tp"),
            P(None, "tp"),
            P("rep", "tp", None),
            P("rep", None, None, "tp"),
            P("rep", None),
            P("rep"),
        ),
        out_specs=(P("rep", "tp"), P("rep", "tp"), P("rep", "tp")),
        check_vma=False,
    )
```

```python
import functools

import jax
import jax.numpy as jnp
from jax import lax
from jax.experimental import pallas as pl
from jax.experimental.pallas import tpu as pltpu
from jax.sharding import PartitionSpec as P

HEAD_SIZE = 128
BLK = 4
LANES = 128
MIB = 1 << 20

adapter_scale = 0.5
masked_score = -1e30


def params(mib):
    return pltpu.CompilerParams(vmem_limit_bytes=mib * MIB)


def cost(flops, moved, exps=0):
    return pl.CostEstimate(flops=flops, bytes_accessed=moved, transcendentals=exps)


def pinned(x):
    return pltpu.with_memory_space_constraint(x, pltpu.HBM)


def iota(shape, dim):
    return lax.broadcasted_iota(jnp.int32, shape, dim)


def pack_kernel(capacity, owner_ref, slot_ref, hidden_ref, out_ref, pick_ref):
    blocks = owner_ref.shape[0]
    rows, width = hidden_ref.shape
    places = out_ref.shape[0]
    square = (blocks, blocks)
    down, across = iota(square, 0), iota(square, 1)
    owner_across = jnp.zeros((1, blocks), jnp.int32)
    owner_down = jnp.zeros((blocks, 1), jnp.int32)
    row_slot = jnp.zeros((rows, 1), jnp.int32)
    for b in range(blocks):
        owner_across = jnp.where(iota((1, blocks), 1) == b, owner_ref[b], owner_across)
        owner_down = jnp.where(iota((blocks, 1), 0) == b, owner_ref[b], owner_down)
        row_slot = jnp.where(iota((rows, 1), 0) // BLK == b, slot_ref[b], row_slot)
    same = (owner_down == owner_across) & (across < down)
    rank = jnp.sum(jnp.where(same, 1.0, 0.0), axis=1, keepdims=True)
    target = owner_down.astype(jnp.float32) * capacity + rank
    spread = iota((blocks, rows), 0) == iota((blocks, rows), 1) // BLK
    row_target = jnp.sum(jnp.where(spread, jnp.broadcast_to(target, (blocks, rows)), 0.0), axis=0, keepdims=True)
    row_target = row_target.astype(jnp.int32) * BLK + iota((1, rows), 1) % BLK
    pick = jnp.where(iota((places, rows), 0) == row_target, 1.0, 0.0).astype(jnp.bfloat16)
    pick_ref[...] = pick
    flags = jnp.where(iota((rows, LANES), 1) == row_slot, 1.0, 0.0).astype(jnp.bfloat16)
    out_ref[:, :width] = jnp.dot(pick, hidden_ref[...], preferred_element_type=jnp.float32).astype(jnp.bfloat16)
    out_ref[:, width:] = jnp.dot(pick, flags, preferred_element_type=jnp.float32).astype(jnp.bfloat16)


def pack(block_owner, block_slot, hidden, replicas, capacity):
    rows, width = hidden.shape
    places = replicas * capacity * BLK
    scalars = pl.BlockSpec(memory_space=pltpu.SMEM)
    return pl.pallas_call(
        functools.partial(pack_kernel, capacity),
        name="pack_rows",
        in_specs=[scalars, scalars, pl.BlockSpec(memory_space=pltpu.VMEM)],
        out_shape=(
            jax.ShapeDtypeStruct((places, width + LANES), jnp.bfloat16),
            jax.ShapeDtypeStruct((places, rows), jnp.bfloat16),
        ),
        compiler_params=params(61),
        cost_estimate=cost(2 * places * rows * width, 2 * (places + rows) * width),
    )(block_owner[:, 0], block_slot, hidden)


def shrink_kernel(rows_ref, shrink_ref, up_hbm, out_ref, flag_ref, up_ref, sem):
    pool, width, rank = shrink_ref.shape
    copy = pltpu.make_async_copy(up_hbm, up_ref, sem)
    copy.start()
    rows = rows_ref[:, :width]
    flag_ref[...] = rows_ref[:, width:]
    total = jnp.zeros(out_ref.shape, jnp.float32)
    for a in range(pool):
        part = jnp.dot(rows, shrink_ref[a], preferred_element_type=jnp.float32)
        total += part * rows_ref[:, width + a : width + a + 1].astype(jnp.float32)
    out_ref[...] = total
    copy.wait()


def shrink(arrived, weights, up):
    places = arrived.shape[0]
    pool, width, rank = weights.shape
    inside, outside = pl.BlockSpec(memory_space=pltpu.VMEM), pl.BlockSpec(memory_space=pltpu.HBM)
    return pl.pallas_call(
        shrink_kernel,
        name="shrink_rows",
        in_specs=[inside, inside, outside],
        out_specs=[inside] * 3,
        out_shape=(
            jax.ShapeDtypeStruct((places, rank), jnp.float32),
            jax.ShapeDtypeStruct((places, LANES), jnp.bfloat16),
            jax.ShapeDtypeStruct(up.shape, up.dtype),
        ),
        scratch_shapes=[pltpu.SemaphoreType.DMA],
        compiler_params=params(8),
        cost_estimate=cost(2 * places * width * rank * pool, 2 * (places * width + weights.size)),
    )(arrived, weights, pinned(up))


def expand_kernel(count, *refs):
    parts, flag_ref, up_ref, out_ref = refs[:count], refs[count], refs[count + 1], refs[count + 2]
    pool, halves, rank, width = up_ref.shape
    total = parts[0][...].astype(jnp.float32)
    for part in parts[1:]:
        total += part[...].astype(jnp.float32)
    shrunk = total.astype(jnp.bfloat16)
    mine = [shrunk * flag_ref[:, a : a + 1] for a in range(pool)]
    table = up_ref[...].reshape(pool * halves * rank, width)
    side = iota(shrunk.shape, 1) // rank
    for half in range(halves):
        wide = jnp.concatenate([jnp.where(side == half, x, jnp.zeros_like(x)) for x in mine], axis=1)
        product = jnp.dot(wide, table, preferred_element_type=jnp.float32)
        out_ref[:, half * width : (half + 1) * width] = (adapter_scale * product).astype(jnp.bfloat16)


def expand(parts, flags, up):
    places = parts[0].shape[0]
    pool, halves, rank, width = up.shape
    return pl.pallas_call(
        functools.partial(expand_kernel, len(parts)),
        name="expand_rows",
        out_shape=jax.ShapeDtypeStruct((places, halves * width), jnp.bfloat16),
        compiler_params=params(8),
        cost_estimate=cost(2 * places * up.size, 2 * up.size + 2 * places * halves * width),
    )(*parts, flags, up)


def cached_kernel(heads, group, length_hbm, query_hbm, key_hbm, value_hbm, shrink_hbm, *refs):
    mean_hbm, lse_ref, shrink_ref, length_ref, query_ref, keys, values, mean_ref, wide_q, wide_o, sems, more = refs
    rows, window, width = keys.shape
    groups = width // HEAD_SIZE
    each = heads // groups
    packed = LANES // heads
    inverse_root = HEAD_SIZE ** (-0.5)

    def copies(i):
        here = pl.ds(i * group, group)
        return (
            pltpu.make_async_copy(key_hbm.at[here], keys.at[here], sems.at[0, i]),
            pltpu.make_async_copy(value_hbm.at[here], values.at[here], sems.at[1, i]),
        )

    ahead = 2
    for i in range(ahead):
        for copy in copies(i):
            copy.start()
    small = [(length_hbm, length_ref), (query_hbm, query_ref), (shrink_hbm, shrink_ref)]
    small = [pltpu.make_async_copy(a, b, more.at[n]) for n, (a, b) in enumerate(small)]
    for copy in small:
        copy.start()
    wide_q[...] = jnp.zeros_like(wide_q)
    lane = iota((window, LANES), 1) // heads
    position = iota((window, LANES), 0)
    sublane = iota((packed, LANES), 0)

    small[0].wait()
    small[1].wait()

    def finished(i):
        here = pl.ds(pl.multiple_of(i * group, group), group)
        return pltpu.make_async_copy(mean_ref.at[here], mean_hbm.at[here], sems.at[2, i])

    def step(i, carry):
        start = pl.multiple_of(i * group, group)
        for h in range(heads):
            part = query_ref[pl.ds(start, group), h * HEAD_SIZE : (h + 1) * HEAD_SIZE]
            wide_q[h // each, pl.ds(h, group, stride=heads), :] = part.astype(jnp.float32)
        key_copy, value_copy = copies(i)
        key_copy.wait()

        @pl.when(i + ahead < rows // group)
        def _():
            for copy in copies(i + ahead):
                copy.start()

        all_weights = []
        for first in range(0, group, packed):
            here = pl.ds(first * heads, LANES)
            query = jnp.concatenate([wide_q[k, here, :] for k in range(groups)], axis=1).astype(jnp.bfloat16)
            block = keys[pl.ds(start + first, packed)].reshape(packed * window, width)
            product = lax.dot_general(block, query, (((1,), (1,)), ((), ())), preferred_element_type=jnp.float32)
            scores = jnp.zeros((window, LANES), jnp.float32)
            limit = jnp.zeros((1, LANES), jnp.int32)
            for r in range(packed):
                scores = jnp.where(lane == r, product[r * window : (r + 1) * window], scores)
                limit = jnp.where(lane[:1] == r, length_ref[start + first + r], limit)
            scores = jnp.where(position < limit, scores * inverse_root, masked_score)
            highest = jnp.max(scores, axis=0, keepdims=True)
            terms = jnp.exp(scores - highest)
            total = jnp.sum(terms, axis=0, keepdims=True)
            all_weights.append(jnp.transpose(terms * (1.0 / total)).astype(jnp.bfloat16))
            logs = jnp.broadcast_to(highest + jnp.log(total), (packed, LANES))
            spread = logs
            for r in range(1, packed):
                spread = jnp.where(sublane == r, pltpu.roll(logs, LANES - r * heads, 1), spread)
            lse_ref[pl.ds(start + first, packed), :] = spread
        value_copy.wait()
        for r in range(0, group, 2):
            weights = all_weights[r // packed][(r % packed) * heads : (r % packed + 2) * heads]
            upper = iota(weights.shape, 0) < heads
            zero = jnp.zeros_like(weights)
            weights = jnp.concatenate([jnp.where(upper, weights, zero), jnp.where(upper, zero, weights)], axis=1)
            block = values[pl.ds(start + r, 2)].reshape(2 * window, width)
            mixed = jnp.dot(weights, block, preferred_element_type=jnp.float32)
            for j in range(2):
                for k in range(groups):
                    mine = pl.ds((r + j) * heads + k * each, each)
                    top = j * heads + k * each
                    wide_o[mine, :] = mixed[top : top + each, k * HEAD_SIZE : (k + 1) * HEAD_SIZE]
        for h in range(heads):
            mean_ref[pl.ds(start, group), h * HEAD_SIZE : (h + 1) * HEAD_SIZE] = wide_o[pl.ds(h, group, stride=heads), :]
        finished(i).start()
        return carry

    lax.fori_loop(0, rows // group, step, 0)
    for i in range(rows // group):
        finished(i).wait()
    small[2].wait()


def cached_attention(lengths, queries, keys, values, weights):
    rows, window, width = keys.shape
    wide = queries.shape[1]
    heads = wide // HEAD_SIZE
    group = max(16, LANES // heads)
    inside, outside = pl.BlockSpec(memory_space=pltpu.VMEM), pl.BlockSpec(memory_space=pltpu.HBM)
    return pl.pallas_call(
        functools.partial(cached_kernel, heads, group),
        name="cached_attention",
        in_specs=[outside] * 5,
        out_specs=[outside, inside, inside],
        scratch_shapes=[
            pltpu.SMEM(lengths.shape, lengths.dtype),
            pltpu.VMEM(queries.shape, queries.dtype),
            pltpu.VMEM(keys.shape, keys.dtype),
            pltpu.VMEM(values.shape, values.dtype),
            pltpu.VMEM((rows, wide), jnp.float32),
            pltpu.VMEM((width // HEAD_SIZE, group * heads, HEAD_SIZE), jnp.float32),
            pltpu.VMEM((group * heads, HEAD_SIZE), jnp.float32),
            pltpu.SemaphoreType.DMA((3, rows // group)),
            pltpu.SemaphoreType.DMA((3,)),
        ],
        out_shape=[
            jax.ShapeDtypeStruct((rows, wide), jnp.float32),
            jax.ShapeDtypeStruct((rows, LANES), jnp.float32),
            jax.ShapeDtypeStruct(weights.shape, weights.dtype),
        ],
        compiler_params=params(20),
        cost_estimate=cost(4 * rows * heads * window * width, 4 * keys.size + 6 * rows * wide, rows * heads * window),
    )(*(pinned(x) for x in (lengths, queries, keys, values, weights)))


def owner_of(place, p, parts):
    return place ^ p if parts == 4 else lax.rem(place + parts - p, parts)


def base_kernel(total, *refs):
    count = total - 1
    pieces, key_hbm, value_hbm, out_ref, last_keys, last_values, keys, values, sems = refs[:count], *refs[count:]
    shard, width = last_keys.shape
    place = lax.axis_index("tp")

    def copies(p):
        rows = pl.ds(pl.multiple_of(owner_of(place, p, total) * shard, shard), shard)
        key_to, value_to = (last_keys, last_values) if p == count else (keys.at[p], values.at[p])
        return (
            pltpu.make_async_copy(key_hbm.at[rows], key_to, sems.at[0, p]),
            pltpu.make_async_copy(value_hbm.at[rows], value_to, sems.at[1, p]),
        )

    for p in range(total):
        for copy in copies(p):
            copy.start()
    for p in range(count):
        for half, (copy, weights) in enumerate(zip(copies(p), (keys, values))):
            here = slice(half * width, (half + 1) * width)
            copy.wait()
            product = jnp.dot(pieces[p][...], weights[p], preferred_element_type=jnp.float32)
            out_ref[:, here] = product if p == 0 else out_ref[:, here] + product
    for copy in copies(count):
        copy.wait()


def base_products(pieces, key_matrix, value_matrix):
    rows, shard = pieces[0].shape
    width = key_matrix.shape[1]
    count = len(pieces)
    inside, outside = pl.BlockSpec(memory_space=pltpu.VMEM), pl.BlockSpec(memory_space=pltpu.HBM)
    last = jax.ShapeDtypeStruct((shard, width), key_matrix.dtype)
    return pl.pallas_call(
        functools.partial(base_kernel, count + 1),
        name="base_products",
        in_specs=[inside] * count + [outside, outside],
        out_specs=[inside] * 3,
        scratch_shapes=[
            pltpu.VMEM((count, shard, width), key_matrix.dtype),
            pltpu.VMEM((count, shard, width), key_matrix.dtype),
            pltpu.SemaphoreType.DMA((2, count + 1)),
        ],
        out_shape=[jax.ShapeDtypeStruct((rows, 2 * width), jnp.float32), last, last],
        compiler_params=params(16),
        cost_estimate=cost(4 * count * rows * shard * width, count * (4 * shard * width + 2 * rows * shard)),
    )(*pieces, pinned(key_matrix), pinned(value_matrix))


def finish_kernel(count, total, *refs):
    late, refs = refs[:count], refs[count:]
    last_keys, last_values, base_ref, back_ref, pick_ref, query_ref, mean_ref, lse_ref = refs[:8]
    new_key_ref, new_value_ref, context_ref = refs[8:]
    rows, wide = query_ref.shape
    width = new_key_ref.shape[1]
    heads = wide // HEAD_SIZE
    each = heads // (width // HEAD_SIZE)
    inverse_root = HEAD_SIZE ** (-0.5)
    delta = lax.dot_general(pick_ref[...], back_ref[...], (((0,), (0,)), ((), ())), preferred_element_type=jnp.float32)
    place = lax.axis_index("tp")
    piece = late[0][...]
    for other in late[1:]:
        piece = jnp.where((place == 0) | (place == total - 1), other[...], piece)
    last = [jnp.dot(piece, w[...], preferred_element_type=jnp.float32) for w in (last_keys, last_values)]
    base = (base_ref[...] + jnp.concatenate(last, axis=1) + delta).astype(jnp.bfloat16)
    new_key_ref[...] = base[:, :width]
    new_value_ref[...] = base[:, width:]
    keys, values = base[:, :width].astype(jnp.float32), base[:, width:].astype(jnp.float32)
    column = iota((rows, LANES), 1)
    own = jnp.zeros((rows, LANES), jnp.float32)
    for h in range(heads):
        k = h // each
        query = query_ref[:, h * HEAD_SIZE : (h + 1) * HEAD_SIZE].astype(jnp.float32)
        score = jnp.sum(query * keys[:, k * HEAD_SIZE : (k + 1) * HEAD_SIZE], axis=1, keepdims=True)
        own = jnp.where(column == h, score * inverse_root, own)
    share = 1.0 / (1.0 + jnp.exp(lse_ref[...] - own))
    for h in range(heads):
        k = h // each
        mean = mean_ref[:, h * HEAD_SIZE : (h + 1) * HEAD_SIZE]
        mixed = mean + share[:, h : h + 1] * (values[:, k * HEAD_SIZE : (k + 1) * HEAD_SIZE] - mean)
        context_ref[:, h * HEAD_SIZE : (h + 1) * HEAD_SIZE] = mixed.astype(jnp.bfloat16)


def finish(late, total, last_keys, last_values, base, back, pick, queries, mean, lse):
    rows, wide = queries.shape
    width = base.shape[1] // 2
    return pl.pallas_call(
        functools.partial(finish_kernel, len(late), total),
        name="finish_rows",
        out_shape=(
            jax.ShapeDtypeStruct((rows, width), jnp.bfloat16),
            jax.ShapeDtypeStruct((rows, width), jnp.bfloat16),
            jax.ShapeDtypeStruct((rows, wide), jnp.bfloat16),
        ),
        compiler_params=params(8),
        cost_estimate=cost(4 * rows * wide, 10 * rows * wide),
    )(*late, last_keys, last_values, base, back, pick, queries, mean, lse)


def swap(x, mask, size):
    return lax.ppermute(x, "tp", [(i, i ^ mask) for i in range(size)])


def turn(x, shift, size):
    return lax.ppermute(x, "tp", [(i, (i + shift) % size) for i in range(size)])


def others(x, size):
    return [turn(x, shift, size) for shift in range(1, size)]


def shards(
    hidden_in,
    queries,
    cache_keys,
    cached_value_rows,
    cache_lengths,
    base_key_matrix,
    base_value_matrix,
    shrink_weights,
    pooled_up_weights,
    block_owner,
    block_slot,
):
    rows_here, shard_width = hidden_in.shape
    replicas = lax.axis_size("rep")
    parts = lax.axis_size("tp")
    blocks_here = rows_here // BLK
    capacity = max(2, (2 * blocks_here + replicas - 1) // replicas)

    def all_to_all(x):
        kept = x.shape
        x = x.reshape(replicas, kept[0] // replicas, kept[1])
        return lax.all_to_all(x, "rep", split_axis=0, concat_axis=0, tiled=True).reshape(kept)

    outgoing, pick = pack(block_owner, block_slot, hidden_in, replicas, capacity)
    arrived = all_to_all(outgoing)

    if parts == 4:
        two = swap(hidden_in, 2, parts)
        one = swap(hidden_in, 1, parts)
    mean, lse, shrink_here = cached_attention(cache_lengths, queries, cache_keys, cached_value_rows, shrink_weights)
    arrived, mean, lse = lax.optimization_barrier((arrived, mean, lse))
    partial_rows, flags, up_here = shrink(arrived, shrink_here, pooled_up_weights)
    if parts == 4:
        paired = partial_rows + swap(partial_rows, 1, parts)
        one, paired = lax.optimization_barrier((one, paired))
        sums = [paired, swap(paired, 2, parts)]
        two, again, *sums = lax.optimization_barrier((two, hidden_in, *sums))
        outer = lax.ppermute(two, "tp", [(1, 0), (2, 3)])
        inner = lax.ppermute(again, "tp", [(1, 2), (2, 1)])
        early, late = [hidden_in, one, two], [inner, outer]
    else:
        sums = [partial_rows] + others(partial_rows, parts)
        pieces = [hidden_in] + others(hidden_in, parts)
        early, late = pieces[:-1], pieces[-1:]
    deltas = expand(sums, flags, up_here)
    back = all_to_all(deltas)
    deltas, *early = lax.optimization_barrier((deltas, *early))
    base, *last = base_products(early, base_key_matrix, base_value_matrix)
    return finish(late, parts, *last, base, back, pick, queries, mean, lse)


def solution(mesh):
    return jax.shard_map(
        shards,
        mesh=mesh,
        in_specs=(
            P("rep", "tp"),
            P("rep", "tp"),
            P("rep", None, "tp"),
            P("rep", None, "tp"),
            P("rep"),
            P(None, "tp"),
            P(None, "tp"),
            P("rep", "tp", None),
            P("rep", None, None, "tp"),
            P("rep", None),
            P("rep"),
        ),
        out_specs=(P("rep", "tp"), P("rep", "tp"), P("rep", "tp")),
        check_vma=False,
    )
```

```python
import functools

import jax
import jax.numpy as jnp
from jax import lax
from jax.experimental import pallas as pl
from jax.experimental.pallas import tpu as pltpu
from jax.sharding import PartitionSpec as P

HEAD_SIZE = 128
BLK = 4
LANES = 128
MIB = 1 << 20

adapter_scale = 0.5
masked_score = -1e30


def params(mib):
    return pltpu.CompilerParams(vmem_limit_bytes=mib * MIB)


def cost(flops, moved, exps=0):
    return pl.CostEstimate(flops=flops, bytes_accessed=moved, transcendentals=exps)


def pinned(x):
    return pltpu.with_memory_space_constraint(x, pltpu.HBM)


def iota(shape, dim):
    return lax.broadcasted_iota(jnp.int32, shape, dim)


def pack_kernel(capacity, owner_ref, slot_ref, hidden_ref, out_ref, pick_ref):
    blocks = owner_ref.shape[0]
    rows, width = hidden_ref.shape
    places = out_ref.shape[0]
    square = (blocks, blocks)
    down, across = iota(square, 0), iota(square, 1)
    owner_across = jnp.zeros((1, blocks), jnp.int32)
    owner_down = jnp.zeros((blocks, 1), jnp.int32)
    row_slot = jnp.zeros((rows, 1), jnp.int32)
    for b in range(blocks):
        owner_across = jnp.where(iota((1, blocks), 1) == b, owner_ref[b], owner_across)
        owner_down = jnp.where(iota((blocks, 1), 0) == b, owner_ref[b], owner_down)
        row_slot = jnp.where(iota((rows, 1), 0) // BLK == b, slot_ref[b], row_slot)
    same = (owner_down == owner_across) & (across < down)
    rank = jnp.sum(jnp.where(same, 1.0, 0.0), axis=1, keepdims=True)
    target = owner_down.astype(jnp.float32) * capacity + rank
    spread = iota((blocks, rows), 0) == iota((blocks, rows), 1) // BLK
    row_target = jnp.sum(jnp.where(spread, jnp.broadcast_to(target, (blocks, rows)), 0.0), axis=0, keepdims=True)
    row_target = row_target.astype(jnp.int32) * BLK + iota((1, rows), 1) % BLK
    pick = jnp.where(iota((places, rows), 0) == row_target, 1.0, 0.0).astype(jnp.bfloat16)
    gather = iota((rows, blocks), 1) == iota((rows, blocks), 0) // BLK
    target = jnp.sum(jnp.where(iota(square, 0) == iota(square, 1), target, 0.0), axis=0, keepdims=True)
    target = jnp.sum(jnp.where(gather, target, 0.0), axis=1, keepdims=True)
    target = target.astype(jnp.int32) * BLK + iota((rows, 1), 0) % BLK
    pick_ref[...] = jnp.where(iota((rows, places), 1) == target, 1.0, 0.0).astype(jnp.bfloat16)
    flags = jnp.where(iota((rows, LANES), 1) == row_slot, 1.0, 0.0).astype(jnp.bfloat16)
    out_ref[:, :width] = jnp.dot(pick, hidden_ref[...], preferred_element_type=jnp.float32).astype(jnp.bfloat16)
    out_ref[:, width:] = jnp.dot(pick, flags, preferred_element_type=jnp.float32).astype(jnp.bfloat16)


def pack(block_owner, block_slot, hidden, replicas, capacity):
    rows, width = hidden.shape
    places = replicas * capacity * BLK
    scalars = pl.BlockSpec(memory_space=pltpu.SMEM)
    return pl.pallas_call(
        functools.partial(pack_kernel, capacity),
        name="pack_rows",
        in_specs=[scalars, scalars, pl.BlockSpec(memory_space=pltpu.VMEM)],
        out_shape=(
            jax.ShapeDtypeStruct((places, width + LANES), jnp.bfloat16),
            jax.ShapeDtypeStruct((rows, places), jnp.bfloat16),
        ),
        compiler_params=params(61),
        cost_estimate=cost(2 * places * rows * width, 2 * (places + rows) * width),
    )(block_owner[:, 0], block_slot, hidden)


def shrink_kernel(rows_ref, shrink_ref, up_hbm, out_ref, sent_ref, flag_ref, up_ref, sem):
    pool, width, rank = shrink_ref.shape
    copy = pltpu.make_async_copy(up_hbm, up_ref, sem)
    copy.start()
    rows = rows_ref[:, :width]
    flag_ref[...] = rows_ref[:, width:]
    total = jnp.zeros(out_ref.shape, jnp.float32)
    for a in range(pool):
        part = jnp.dot(rows, shrink_ref[a], preferred_element_type=jnp.float32)
        total += part * rows_ref[:, width + a : width + a + 1].astype(jnp.float32)
    out_ref[...] = total
    sent_ref[...] = total.astype(jnp.bfloat16)
    copy.wait()


def shrink(arrived, weights, up):
    places = arrived.shape[0]
    pool, width, rank = weights.shape
    inside, outside = pl.BlockSpec(memory_space=pltpu.VMEM), pl.BlockSpec(memory_space=pltpu.HBM)
    return pl.pallas_call(
        shrink_kernel,
        name="shrink_rows",
        in_specs=[inside, inside, outside],
        out_specs=[inside] * 4,
        out_shape=(
            jax.ShapeDtypeStruct((places, rank), jnp.float32),
            jax.ShapeDtypeStruct((places, rank), jnp.bfloat16),
            jax.ShapeDtypeStruct((places, LANES), jnp.bfloat16),
            jax.ShapeDtypeStruct(up.shape, up.dtype),
        ),
        scratch_shapes=[pltpu.SemaphoreType.DMA],
        compiler_params=params(8),
        cost_estimate=cost(2 * places * width * rank * pool, 2 * (places * width + weights.size)),
    )(arrived, weights, pinned(up))


def expand_kernel(count, *refs):
    parts, flag_ref, up_ref, out_ref = refs[:count], refs[count], refs[count + 1], refs[count + 2]
    pool, halves, rank, width = up_ref.shape
    total = parts[0][...].astype(jnp.float32)
    for part in parts[1:]:
        total += part[...].astype(jnp.float32)
    shrunk = total.astype(jnp.bfloat16)
    mine = [shrunk * flag_ref[:, a : a + 1] for a in range(pool)]
    table = up_ref[...].reshape(pool * halves * rank, width)
    side = iota(shrunk.shape, 1) // rank
    for half in range(halves):
        wide = jnp.concatenate([jnp.where(side == half, x, jnp.zeros_like(x)) for x in mine], axis=1)
        product = jnp.dot(wide, table, preferred_element_type=jnp.float32)
        out_ref[:, half * width : (half + 1) * width] = (adapter_scale * product).astype(jnp.bfloat16)


def expand(parts, flags, up):
    places = parts[0].shape[0]
    pool, halves, rank, width = up.shape
    return pl.pallas_call(
        functools.partial(expand_kernel, len(parts)),
        name="expand_rows",
        out_shape=jax.ShapeDtypeStruct((places, halves * width), jnp.bfloat16),
        compiler_params=params(8),
        cost_estimate=cost(2 * places * up.size, 2 * up.size + 2 * places * halves * width),
    )(*parts, flags, up)


def cached_kernel(heads, group, length_hbm, query_hbm, key_hbm, value_hbm, shrink_hbm, *refs):
    groups = key_hbm.shape[2] // HEAD_SIZE
    mean_hbm, lse_ref, shrink_ref, length_ref, query_ref, keys, values, mean_ref, wide_q, wide_o, sems, more = refs
    rows, window, width = keys.shape
    each = heads // groups
    packed = LANES // heads
    inverse_root = HEAD_SIZE ** (-0.5)

    def copies(i):
        here = pl.ds(i * group, group)
        return (
            pltpu.make_async_copy(key_hbm.at[here], keys.at[here], sems.at[0, i]),
            pltpu.make_async_copy(value_hbm.at[here], values.at[here], sems.at[1, i]),
        )

    ahead = 2
    for i in range(ahead):
        for copy in copies(i):
            copy.start()
    small = [(length_hbm, length_ref), (query_hbm, query_ref), (shrink_hbm, shrink_ref)]
    small = [pltpu.make_async_copy(a, b, more.at[n]) for n, (a, b) in enumerate(small)]
    for copy in small:
        copy.start()
    wide_q[...] = jnp.zeros_like(wide_q)
    lane = iota((window, LANES), 1) // heads
    position = iota((window, LANES), 0)
    sublane = iota((packed, LANES), 0)

    small[0].wait()
    small[1].wait()

    def finished(i):
        here = pl.ds(pl.multiple_of(i * group, group), group)
        return pltpu.make_async_copy(mean_ref.at[here], mean_hbm.at[here], sems.at[2, i])

    def step(i, carry):
        start = pl.multiple_of(i * group, group)
        for h in range(heads):
            part = query_ref[pl.ds(start, group), h * HEAD_SIZE : (h + 1) * HEAD_SIZE]
            wide_q[h // each, pl.ds(h, group, stride=heads), :] = part.astype(jnp.float32)
        key_copy, value_copy = copies(i)
        key_copy.wait()

        @pl.when(i + ahead < rows // group)
        def _():
            for copy in copies(i + ahead):
                copy.start()

        all_weights = []
        for first in range(0, group, packed):
            here = pl.ds(first * heads, LANES)
            query = jnp.concatenate([wide_q[k, here, :] for k in range(groups)], axis=1).astype(jnp.bfloat16)
            block = keys[pl.ds(start + first, packed)].reshape(packed * window, width)
            product = lax.dot_general(block, query, (((1,), (1,)), ((), ())), preferred_element_type=jnp.float32)
            scores = jnp.zeros((window, LANES), jnp.float32)
            limit = jnp.zeros((1, LANES), jnp.int32)
            for r in range(packed):
                scores = jnp.where(lane == r, product[r * window : (r + 1) * window], scores)
                limit = jnp.where(lane[:1] == r, length_ref[start + first + r], limit)
            scores = jnp.where(position < limit, scores * inverse_root, masked_score)
            highest = jnp.max(scores, axis=0, keepdims=True)
            terms = jnp.exp(scores - highest)
            total = jnp.sum(terms, axis=0, keepdims=True)
            all_weights.append(jnp.transpose(terms * (1.0 / total)).astype(jnp.bfloat16))
            logs = jnp.broadcast_to(highest + jnp.log(total), (packed, LANES))
            spread = logs
            for r in range(1, packed):
                spread = jnp.where(sublane == r, pltpu.roll(logs, LANES - r * heads, 1), spread)
            lse_ref[pl.ds(start + first, packed), :] = spread
        value_copy.wait()
        for r in range(0, group, 2):
            weights = all_weights[r // packed][(r % packed) * heads : (r % packed + 2) * heads]
            upper = iota(weights.shape, 0) < heads
            zero = jnp.zeros_like(weights)
            weights = jnp.concatenate([jnp.where(upper, weights, zero), jnp.where(upper, zero, weights)], axis=1)
            block = values[pl.ds(start + r, 2)].reshape(2 * window, width)
            mixed = jnp.dot(weights, block, preferred_element_type=jnp.float32)
            for j in range(2):
                for k in range(groups):
                    mine = pl.ds((r + j) * heads + k * each, each)
                    top = j * heads + k * each
                    wide_o[mine, :] = mixed[top : top + each, k * HEAD_SIZE : (k + 1) * HEAD_SIZE]
        for h in range(heads):
            mean_ref[pl.ds(start, group), h * HEAD_SIZE : (h + 1) * HEAD_SIZE] = wide_o[pl.ds(h, group, stride=heads), :]
        finished(i).start()
        return carry

    lax.fori_loop(0, rows // group, step, 0)
    for i in range(rows // group):
        finished(i).wait()
    small[2].wait()


def cached_attention(lengths, queries, keys, values, weights):
    rows, window, width = keys.shape
    wide = queries.shape[1]
    heads = wide // HEAD_SIZE
    group = max(16, LANES // heads)
    groups = width // HEAD_SIZE
    inside, outside = pl.BlockSpec(memory_space=pltpu.VMEM), pl.BlockSpec(memory_space=pltpu.HBM)
    return pl.pallas_call(
        functools.partial(cached_kernel, heads, group),
        name="cached_attention",
        in_specs=[outside] * 5,
        out_specs=[outside, inside, inside],
        scratch_shapes=[
            pltpu.SMEM(lengths.shape, lengths.dtype),
            pltpu.VMEM(queries.shape, queries.dtype),
            pltpu.VMEM(keys.shape, keys.dtype),
            pltpu.VMEM(values.shape, values.dtype),
            pltpu.VMEM((rows, wide), jnp.float32),
            pltpu.VMEM((groups, group * heads, HEAD_SIZE), jnp.float32),
            pltpu.VMEM((group * heads, HEAD_SIZE), jnp.float32),
            pltpu.SemaphoreType.DMA((3, rows // group)),
            pltpu.SemaphoreType.DMA((3,)),
        ],
        out_shape=[
            pltpu.HBM((rows, wide), jnp.float32),
            jax.ShapeDtypeStruct((rows, LANES), jnp.float32),
            jax.ShapeDtypeStruct(weights.shape, weights.dtype),
        ],
        compiler_params=params(20),
        cost_estimate=cost(4 * rows * heads * window * width, 4 * keys.size + 6 * rows * wide, rows * heads * window),
    )(*(pinned(x) for x in (lengths, queries, keys, values, weights)))


def owner_of(place, p, parts):
    return place ^ p if parts == 4 else lax.rem(place + parts - p, parts)


def base_kernel(total, *refs):
    count = total - 1
    pieces, key_hbm, value_hbm, out_ref, last_keys, last_values, keys, values, sems = refs[:count], *refs[count:]
    shard, width = last_keys.shape
    place = lax.axis_index("tp")

    def copies(p):
        rows = pl.ds(pl.multiple_of(owner_of(place, p, total) * shard, shard), shard)
        key_to, value_to = (last_keys, last_values) if p == count else (keys.at[p], values.at[p])
        return (
            pltpu.make_async_copy(key_hbm.at[rows], key_to, sems.at[0, p]),
            pltpu.make_async_copy(value_hbm.at[rows], value_to, sems.at[1, p]),
        )

    for p in range(total):
        for copy in copies(p):
            copy.start()
    for p in range(count):
        for half, (copy, weights) in enumerate(zip(copies(p), (keys, values))):
            here = slice(half * width, (half + 1) * width)
            copy.wait()
            product = jnp.dot(pieces[p][...], weights[p], preferred_element_type=jnp.float32)
            out_ref[:, here] = product if p == 0 else out_ref[:, here] + product
    for copy in copies(count):
        copy.wait()


def base_products(pieces, key_matrix, value_matrix):
    rows, shard = pieces[0].shape
    width = key_matrix.shape[1]
    count = len(pieces)
    inside, outside = pl.BlockSpec(memory_space=pltpu.VMEM), pl.BlockSpec(memory_space=pltpu.HBM)
    last = jax.ShapeDtypeStruct((shard, width), key_matrix.dtype)
    return pl.pallas_call(
        functools.partial(base_kernel, count + 1),
        name="base_products",
        in_specs=[inside] * count + [outside, outside],
        out_specs=[inside] * 3,
        scratch_shapes=[
            pltpu.VMEM((count, shard, width), key_matrix.dtype),
            pltpu.VMEM((count, shard, width), key_matrix.dtype),
            pltpu.SemaphoreType.DMA((2, count + 1)),
        ],
        out_shape=[jax.ShapeDtypeStruct((rows, 2 * width), jnp.float32), last, last],
        compiler_params=params(16),
        cost_estimate=cost(4 * count * rows * shard * width, count * (4 * shard * width + 2 * rows * shard)),
    )(*pieces, pinned(key_matrix), pinned(value_matrix))


def last_kernel(count, total, *refs):
    sources, (keys, values, base_ref, out_ref, piece_ref, sem) = refs[:count], refs[count:]
    width = keys.shape[1]
    place = lax.axis_index("tp")
    outer = (place == 0) | (place == total - 1)
    for n, source in enumerate(sources):

        @pl.when(True if count == 1 else outer == (n == count - 1))
        def _():
            copy = pltpu.make_async_copy(source, piece_ref, sem)
            copy.start()
            copy.wait()

    for half, weights in enumerate((keys, values)):
        here = slice(half * width, (half + 1) * width)
        out_ref[:, here] = base_ref[:, here] + jnp.dot(piece_ref[...], weights[...], preferred_element_type=jnp.float32)


def last_product(late, total, keys, values, base):
    inside, outside = pl.BlockSpec(memory_space=pltpu.VMEM), pl.BlockSpec(memory_space=pltpu.HBM)
    return pl.pallas_call(
        functools.partial(last_kernel, len(late), total),
        name="last_product",
        in_specs=[outside] * len(late) + [inside] * 3,
        out_specs=inside,
        out_shape=jax.ShapeDtypeStruct(base.shape, base.dtype),
        scratch_shapes=[pltpu.VMEM(late[0].shape, late[0].dtype), pltpu.SemaphoreType.DMA],
        compiler_params=params(8),
        cost_estimate=cost(2 * late[0].size * base.shape[1], 4 * keys.size),
    )(*late, keys, values, base)


def finish_kernel(base_ref, back_ref, pick_ref, query_ref, lse_ref, mean_hbm, *refs):
    new_key_ref, new_value_ref, context_hbm, mean_ref, context_ref, sems = refs
    rows, wide = query_ref.shape
    width = new_key_ref.shape[1]
    heads = wide // HEAD_SIZE
    groups = width // HEAD_SIZE
    each = heads // groups
    inverse_root = HEAD_SIZE ** (-0.5)
    mean_copy = pltpu.make_async_copy(mean_hbm, mean_ref, sems.at[groups])
    mean_copy.start()
    delta = jnp.dot(pick_ref[...], back_ref[...], preferred_element_type=jnp.float32)
    base = (base_ref[...] + delta).astype(jnp.bfloat16)
    new_key_ref[...] = base[:, :width]
    new_value_ref[...] = base[:, width:]
    keys, values = base[:, :width].astype(jnp.float32), base[:, width:].astype(jnp.float32)
    column = iota((rows, LANES), 1)
    own = jnp.zeros((rows, LANES), jnp.float32)
    for h in range(heads):
        k = h // each
        query = query_ref[:, h * HEAD_SIZE : (h + 1) * HEAD_SIZE].astype(jnp.float32)
        score = jnp.sum(query * keys[:, k * HEAD_SIZE : (k + 1) * HEAD_SIZE], axis=1, keepdims=True)
        own = jnp.where(column == h, score * inverse_root, own)
    share = 1.0 / (1.0 + jnp.exp(lse_ref[...] - own))
    mean_copy.wait()
    for k in range(groups):
        for h in range(k * each, (k + 1) * each):
            mean = mean_ref[:, h * HEAD_SIZE : (h + 1) * HEAD_SIZE]
            mixed = mean + share[:, h : h + 1] * (values[:, k * HEAD_SIZE : (k + 1) * HEAD_SIZE] - mean)
            context_ref[:, h * HEAD_SIZE : (h + 1) * HEAD_SIZE] = mixed.astype(jnp.bfloat16)
        part = pl.ds(k * each * HEAD_SIZE, each * HEAD_SIZE)
        pltpu.make_async_copy(context_ref.at[:, part], context_hbm.at[:, part], sems.at[k]).start()
    for k in range(groups):
        part = pl.ds(k * each * HEAD_SIZE, each * HEAD_SIZE)
        pltpu.make_async_copy(context_ref.at[:, part], context_hbm.at[:, part], sems.at[k]).wait()


def finish(base, back, pick, queries, lse, mean):
    rows, wide = queries.shape
    width = base.shape[1] // 2
    inside, outside = pl.BlockSpec(memory_space=pltpu.VMEM), pl.BlockSpec(memory_space=pltpu.HBM)
    return pl.pallas_call(
        finish_kernel,
        name="finish_rows",
        in_specs=[inside] * 5 + [outside],
        out_specs=[inside, inside, outside],
        out_shape=(
            jax.ShapeDtypeStruct((rows, width), jnp.bfloat16),
            jax.ShapeDtypeStruct((rows, width), jnp.bfloat16),
            jax.ShapeDtypeStruct((rows, wide), jnp.bfloat16),
        ),
        scratch_shapes=[
            pltpu.VMEM(mean.shape, mean.dtype),
            pltpu.VMEM((rows, wide), jnp.bfloat16),
            pltpu.SemaphoreType.DMA((width // HEAD_SIZE + 1,)),
        ],
        compiler_params=params(8),
        cost_estimate=cost(4 * rows * wide, 10 * rows * wide),
    )(base, back, pick, queries, lse, pinned(mean))


def swap(x, mask, size):
    return lax.ppermute(x, "tp", [(i, i ^ mask) for i in range(size)])


def turn(x, shift, size):
    return lax.ppermute(x, "tp", [(i, (i + shift) % size) for i in range(size)])


def others(x, size):
    return [turn(x, shift, size) for shift in range(1, size)]


def shards(
    hidden_in,
    queries,
    cache_keys,
    cached_value_rows,
    cache_lengths,
    base_key_matrix,
    base_value_matrix,
    shrink_weights,
    pooled_up_weights,
    block_owner,
    block_slot,
):
    rows_here, shard_width = hidden_in.shape
    replicas = lax.axis_size("rep")
    parts = lax.axis_size("tp")
    blocks_here = rows_here // BLK
    capacity = max(2, (2 * blocks_here + replicas - 1) // replicas)

    def all_to_all(x):
        kept = x.shape
        x = x.reshape(replicas, kept[0] // replicas, kept[1])
        return lax.all_to_all(x, "rep", split_axis=0, concat_axis=0, tiled=True).reshape(kept)

    outgoing, pick = pack(block_owner, block_slot, hidden_in, replicas, capacity)
    arrived = all_to_all(outgoing)

    if parts == 4:
        one = swap(hidden_in, 1, parts)
        two = swap(hidden_in, 2, parts)
    mean, lse, shrink_here = cached_attention(cache_lengths, queries, cache_keys, cached_value_rows, shrink_weights)
    arrived, lse = lax.optimization_barrier((arrived, lse))
    partial_rows, sent, flags, up_here = shrink(arrived, shrink_here, pooled_up_weights)
    if parts == 4:
        paired = partial_rows + swap(sent, 1, parts).astype(jnp.float32)
        one, paired = lax.optimization_barrier((one, paired))
        sums = [paired, swap(paired.astype(jnp.bfloat16), 2, parts)]
        two, again, *sums = lax.optimization_barrier((two, hidden_in, *sums))
        outer = lax.ppermute(two, "tp", [(1, 0), (2, 3)])
        inner = lax.ppermute(again, "tp", [(1, 2), (2, 1)])
        early, late = [hidden_in, one, two], [inner, outer]
    else:
        sums = [partial_rows] + others(sent, parts)
        pieces = [hidden_in] + others(hidden_in, parts)
        early, late = pieces[:-1], pieces[-1:]
    deltas = expand(sums, flags, up_here)
    back = all_to_all(deltas)
    deltas, *early = lax.optimization_barrier((deltas, *early))
    base, *last = base_products(early, base_key_matrix, base_value_matrix)
    base = last_product(late, parts, *last, base)
    return finish(base, back, pick, queries, lse, mean)


def solution(mesh):
    return jax.shard_map(
        shards,
        mesh=mesh,
        in_specs=(
            P("rep", "tp"),
            P("rep", "tp"),
            P("rep", None, "tp"),
            P("rep", None, "tp"),
            P("rep"),
            P(None, "tp"),
            P(None, "tp"),
            P("rep", "tp", None),
            P("rep", None, None, "tp"),
            P("rep", None),
            P("rep"),
        ),
        out_specs=(P("rep", "tp"), P("rep", "tp"), P("rep", "tp")),
        check_vma=False,
    )
```

```python
import functools

import jax
import jax.numpy as jnp
from jax import lax
from jax.experimental import pallas as pl
from jax.experimental.pallas import tpu as pltpu
from jax.sharding import PartitionSpec as P

HEAD_SIZE = 128
BLK = 4
LANES = 128
MIB = 1 << 20

adapter_scale = 0.5
masked_score = -1e30


def params(mib):
    return pltpu.CompilerParams(vmem_limit_bytes=mib * MIB)


def cost(flops, moved, exps=0):
    return pl.CostEstimate(flops=flops, bytes_accessed=moved, transcendentals=exps)


def pinned(x):
    return pltpu.with_memory_space_constraint(x, pltpu.HBM)


def iota(shape, dim):
    return lax.broadcasted_iota(jnp.int32, shape, dim)


def pack_kernel(capacity, owner_ref, slot_ref, hidden_ref, out_ref, pick_ref):
    blocks = owner_ref.shape[0]
    rows, width = hidden_ref.shape
    places = out_ref.shape[0]
    square = (blocks, blocks)
    down, across = iota(square, 0), iota(square, 1)
    owner_across = jnp.zeros((1, blocks), jnp.int32)
    owner_down = jnp.zeros((blocks, 1), jnp.int32)
    row_slot = jnp.zeros((rows, 1), jnp.int32)
    for b in range(blocks):
        owner_across = jnp.where(iota((1, blocks), 1) == b, owner_ref[b], owner_across)
        owner_down = jnp.where(iota((blocks, 1), 0) == b, owner_ref[b], owner_down)
        row_slot = jnp.where(iota((rows, 1), 0) // BLK == b, slot_ref[b], row_slot)
    same = (owner_down == owner_across) & (across < down)
    rank = jnp.sum(jnp.where(same, 1.0, 0.0), axis=1, keepdims=True)
    target = owner_down.astype(jnp.float32) * capacity + rank
    spread = iota((blocks, rows), 0) == iota((blocks, rows), 1) // BLK
    row_target = jnp.sum(jnp.where(spread, jnp.broadcast_to(target, (blocks, rows)), 0.0), axis=0, keepdims=True)
    row_target = row_target.astype(jnp.int32) * BLK + iota((1, rows), 1) % BLK
    pick = jnp.where(iota((places, rows), 0) == row_target, 1.0, 0.0).astype(jnp.bfloat16)
    gather = iota((rows, blocks), 1) == iota((rows, blocks), 0) // BLK
    target = jnp.sum(jnp.where(iota(square, 0) == iota(square, 1), target, 0.0), axis=0, keepdims=True)
    target = jnp.sum(jnp.where(gather, target, 0.0), axis=1, keepdims=True)
    target = target.astype(jnp.int32) * BLK + iota((rows, 1), 0) % BLK
    pick_ref[...] = jnp.where(iota((rows, places), 1) == target, 1.0, 0.0).astype(jnp.bfloat16)
    flags = jnp.where(iota((rows, LANES), 1) == row_slot, 1.0, 0.0).astype(jnp.bfloat16)
    out_ref[:, :width] = jnp.dot(pick, hidden_ref[...], preferred_element_type=jnp.float32).astype(jnp.bfloat16)
    out_ref[:, width:] = jnp.dot(pick, flags, preferred_element_type=jnp.float32).astype(jnp.bfloat16)


def pack(block_owner, block_slot, hidden, replicas, capacity):
    rows, width = hidden.shape
    places = replicas * capacity * BLK
    scalars = pl.BlockSpec(memory_space=pltpu.SMEM)
    return pl.pallas_call(
        functools.partial(pack_kernel, capacity),
        name="pack_rows",
        in_specs=[scalars, scalars, pl.BlockSpec(memory_space=pltpu.VMEM)],
        out_shape=(
            jax.ShapeDtypeStruct((places, width + LANES), jnp.bfloat16),
            jax.ShapeDtypeStruct((rows, places), jnp.bfloat16),
        ),
        compiler_params=params(61),
        cost_estimate=cost(2 * places * rows * width, 2 * (places + rows) * width),
    )(block_owner[:, 0], block_slot, hidden)


def shrink_kernel(rows_ref, shrink_ref, out_ref, sent_ref, flag_ref):
    pool, width, rank = shrink_ref.shape
    rows = rows_ref[:, :width]
    flag_ref[...] = rows_ref[:, width:]
    total = jnp.zeros(out_ref.shape, jnp.float32)
    for a in range(pool):
        part = jnp.dot(rows, shrink_ref[a], preferred_element_type=jnp.float32)
        total += part * rows_ref[:, width + a : width + a + 1].astype(jnp.float32)
    out_ref[...] = total
    sent_ref[...] = total.astype(jnp.bfloat16)


def shrink(arrived, weights):
    places = arrived.shape[0]
    pool, width, rank = weights.shape
    return pl.pallas_call(
        shrink_kernel,
        name="shrink_rows",
        out_shape=(
            jax.ShapeDtypeStruct((places, rank), jnp.float32),
            jax.ShapeDtypeStruct((places, rank), jnp.bfloat16),
            jax.ShapeDtypeStruct((places, LANES), jnp.bfloat16),
        ),
        compiler_params=params(8),
        cost_estimate=cost(2 * places * width * rank * pool, 2 * (places * width + weights.size)),
    )(arrived, weights)


def expand_kernel(count, *refs):
    parts, flag_ref, up_ref, out_ref = refs[:count], *refs[count:]
    pool, halves, rank, width = up_ref.shape
    total = parts[0][...].astype(jnp.float32)
    for part in parts[1:]:
        total += part[...].astype(jnp.float32)
    shrunk = total.astype(jnp.bfloat16)
    mine = [shrunk * flag_ref[:, a : a + 1] for a in range(pool)]
    side = iota(shrunk.shape, 1) // rank
    wide = [
        jnp.concatenate([jnp.where(side == half, x, jnp.zeros_like(x)) for x in mine], axis=1) for half in range(halves)
    ]
    table = up_ref[...].reshape(pool * halves * rank, width)
    for half in range(halves):
        product = jnp.dot(wide[half], table, preferred_element_type=jnp.float32)
        out_ref[:, half * width : (half + 1) * width] = (adapter_scale * product).astype(jnp.bfloat16)


def expand(parts, flags, up):
    places = parts[0].shape[0]
    pool, halves, rank, width = up.shape
    return pl.pallas_call(
        functools.partial(expand_kernel, len(parts)),
        name="expand_rows",
        out_shape=jax.ShapeDtypeStruct((places, halves * width), jnp.bfloat16),
        compiler_params=params(8),
        cost_estimate=cost(2 * places * up.size, 2 * up.size + 2 * places * halves * width),
    )(*parts, flags, up)


def cached_kernel(heads, group, length_hbm, query_hbm, key_hbm, value_hbm, shrink_hbm, *refs):
    groups = key_hbm.shape[2] // HEAD_SIZE
    mean_hbm, lse_ref, shrink_ref, length_ref, query_ref, keys, values, mean_ref, wide_q, wide_o, sems, more = refs
    rows, window, width = keys.shape
    each = heads // groups
    packed = LANES // heads
    inverse_root = HEAD_SIZE ** (-0.5)

    def copies(i):
        here = pl.ds(i * group, group)
        return (
            pltpu.make_async_copy(key_hbm.at[here], keys.at[here], sems.at[0, i]),
            pltpu.make_async_copy(value_hbm.at[here], values.at[here], sems.at[1, i]),
        )

    ahead = 2
    for i in range(ahead):
        for copy in copies(i):
            copy.start()
    small = [(length_hbm, length_ref), (query_hbm, query_ref), (shrink_hbm, shrink_ref)]
    small = [pltpu.make_async_copy(a, b, more.at[n]) for n, (a, b) in enumerate(small)]
    for copy in small:
        copy.start()
    wide_q[...] = jnp.zeros_like(wide_q)
    lane = iota((window, LANES), 1) // heads
    position = iota((window, LANES), 0)
    sublane = iota((packed, LANES), 0)

    small[0].wait()
    small[1].wait()

    def finished(i):
        here = pl.ds(pl.multiple_of(i * group, group), group)
        return pltpu.make_async_copy(mean_ref.at[here], mean_hbm.at[here], sems.at[2, i])

    def step(i, carry):
        start = pl.multiple_of(i * group, group)
        for h in range(heads):
            part = query_ref[pl.ds(start, group), h * HEAD_SIZE : (h + 1) * HEAD_SIZE]
            wide_q[h // each, pl.ds(h, group, stride=heads), :] = part.astype(jnp.float32)
        key_copy, value_copy = copies(i)
        key_copy.wait()

        @pl.when(i + ahead < rows // group)
        def _():
            for copy in copies(i + ahead):
                copy.start()

        all_weights = []
        for first in range(0, group, packed):
            here = pl.ds(first * heads, LANES)
            query = jnp.concatenate([wide_q[k, here, :] for k in range(groups)], axis=1).astype(jnp.bfloat16)
            block = keys[pl.ds(start + first, packed)].reshape(packed * window, width)
            product = lax.dot_general(block, query, (((1,), (1,)), ((), ())), preferred_element_type=jnp.float32)
            scores = jnp.zeros((window, LANES), jnp.float32)
            limit = jnp.zeros((1, LANES), jnp.int32)
            for r in range(packed):
                scores = jnp.where(lane == r, product[r * window : (r + 1) * window], scores)
                limit = jnp.where(lane[:1] == r, length_ref[start + first + r], limit)
            scores = jnp.where(position < limit, scores * inverse_root, masked_score)
            highest = jnp.max(scores, axis=0, keepdims=True)
            terms = jnp.exp(scores - highest)
            total = jnp.sum(terms, axis=0, keepdims=True)
            all_weights.append(jnp.transpose(terms * (1.0 / total)).astype(jnp.bfloat16))
            logs = jnp.broadcast_to(highest + jnp.log(total), (packed, LANES))
            spread = logs
            for r in range(1, packed):
                spread = jnp.where(sublane == r, pltpu.roll(logs, LANES - r * heads, 1), spread)
            lse_ref[pl.ds(start + first, packed), :] = spread
        value_copy.wait()
        for r in range(0, group, 2):
            weights = all_weights[r // packed][(r % packed) * heads : (r % packed + 2) * heads]
            upper = iota(weights.shape, 0) < heads
            zero = jnp.zeros_like(weights)
            weights = jnp.concatenate([jnp.where(upper, weights, zero), jnp.where(upper, zero, weights)], axis=1)
            block = values[pl.ds(start + r, 2)].reshape(2 * window, width)
            mixed = jnp.dot(weights, block, preferred_element_type=jnp.float32)
            for j in range(2):
                for k in range(groups):
                    mine = pl.ds((r + j) * heads + k * each, each)
                    top = j * heads + k * each
                    wide_o[mine, :] = mixed[top : top + each, k * HEAD_SIZE : (k + 1) * HEAD_SIZE]
        for h in range(heads):
            mean_ref[pl.ds(start, group), h * HEAD_SIZE : (h + 1) * HEAD_SIZE] = wide_o[pl.ds(h, group, stride=heads), :]
        finished(i).start()
        return carry

    lax.fori_loop(0, rows // group, step, 0)
    for i in range(rows // group):
        finished(i).wait()
    small[2].wait()


def cached_attention(lengths, queries, keys, values, weights):
    rows, window, width = keys.shape
    wide = queries.shape[1]
    heads = wide // HEAD_SIZE
    group = max(16, LANES // heads)
    groups = width // HEAD_SIZE
    inside, outside = pl.BlockSpec(memory_space=pltpu.VMEM), pl.BlockSpec(memory_space=pltpu.HBM)
    return pl.pallas_call(
        functools.partial(cached_kernel, heads, group),
        name="cached_attention",
        in_specs=[outside] * 5,
        out_specs=[outside, inside, inside],
        scratch_shapes=[
            pltpu.SMEM(lengths.shape, lengths.dtype),
            pltpu.VMEM(queries.shape, queries.dtype),
            pltpu.VMEM(keys.shape, keys.dtype),
            pltpu.VMEM(values.shape, values.dtype),
            pltpu.VMEM((rows, wide), jnp.float32),
            pltpu.VMEM((groups, group * heads, HEAD_SIZE), jnp.float32),
            pltpu.VMEM((group * heads, HEAD_SIZE), jnp.float32),
            pltpu.SemaphoreType.DMA((3, rows // group)),
            pltpu.SemaphoreType.DMA((3,)),
        ],
        out_shape=[
            pltpu.HBM((rows, wide), jnp.float32),
            jax.ShapeDtypeStruct((rows, LANES), jnp.float32),
            jax.ShapeDtypeStruct(weights.shape, weights.dtype),
        ],
        compiler_params=params(20),
        cost_estimate=cost(4 * rows * heads * window * width, 4 * keys.size + 6 * rows * wide, rows * heads * window),
    )(*(pinned(x) for x in (lengths, queries, keys, values, weights)))


def owner_of(place, p, parts):
    return place ^ p if parts == 4 else lax.rem(place + parts - p, parts)


def own_kernel(total, piece_ref, key_hbm, value_hbm, up_hbm, out_ref, up_ref, keys, values, sems):
    shard, width = keys.shape
    rows = pl.ds(pl.multiple_of(owner_of(lax.axis_index("tp"), 0, total) * shard, shard), shard)
    copies = [
        pltpu.make_async_copy(key_hbm.at[rows], keys, sems.at[0]),
        pltpu.make_async_copy(value_hbm.at[rows], values, sems.at[1]),
        pltpu.make_async_copy(up_hbm, up_ref, sems.at[2]),
    ]
    for copy in copies:
        copy.start()
    for half, weights in enumerate((keys, values)):
        copies[half].wait()
        product = jnp.dot(piece_ref[...], weights[...], preferred_element_type=jnp.float32)
        out_ref[:, half * width : (half + 1) * width] = product
    copies[2].wait()


def own_product(piece, total, key_matrix, value_matrix, up):
    rows, shard = piece.shape
    width = key_matrix.shape[1]
    inside, outside = pl.BlockSpec(memory_space=pltpu.VMEM), pl.BlockSpec(memory_space=pltpu.HBM)
    return pl.pallas_call(
        functools.partial(own_kernel, total),
        name="own_product",
        in_specs=[inside, outside, outside, outside],
        out_specs=[inside, inside],
        out_shape=[jax.ShapeDtypeStruct((rows, 2 * width), jnp.float32), jax.ShapeDtypeStruct(up.shape, up.dtype)],
        scratch_shapes=[pltpu.VMEM((shard, width), key_matrix.dtype)] * 2 + [pltpu.SemaphoreType.DMA((3,))],
        compiler_params=params(8),
        cost_estimate=cost(4 * rows * shard * width, 4 * shard * width),
    )(piece, pinned(key_matrix), pinned(value_matrix), pinned(up))


def base_kernel(total, *refs):
    count = total - 2
    pieces, refs = refs[:count], refs[count:]
    so_far, key_hbm, value_hbm, mean_hbm, out_ref, last_keys, last_values, mean_ref, keys, values, sems = refs
    shard, width = last_keys.shape
    place = lax.axis_index("tp")

    def copies(p):
        rows = pl.ds(pl.multiple_of(owner_of(place, p + 1, total) * shard, shard), shard)
        key_to, value_to = (last_keys, last_values) if p == count else (keys.at[p], values.at[p])
        key_copy = pltpu.make_async_copy(key_hbm.at[rows], key_to, sems.at[0, p]) if p > 0 else None
        return key_copy, pltpu.make_async_copy(value_hbm.at[rows], value_to, sems.at[1, p])

    everything = [copy for p in range(count + 1) for copy in copies(p) if copy is not None]
    everything.append(pltpu.make_async_copy(mean_hbm, mean_ref, sems.at[0, 0]))
    for copy in everything:
        copy.start()
    out_ref[...] = so_far[...]
    for p in range(count):
        for half, (copy, weights) in enumerate(zip(copies(p), (keys, values))):
            if copy is None:
                continue
            here = slice(half * width, (half + 1) * width)
            copy.wait()
            out_ref[:, here] += jnp.dot(pieces[p][...], weights[p], preferred_element_type=jnp.float32)
    for copy in everything[-3:]:
        copy.wait()


def base_products(pieces, so_far, key_matrix, value_matrix, mean):
    rows, shard = pieces[0].shape
    width = key_matrix.shape[1]
    count = len(pieces)
    inside, outside = pl.BlockSpec(memory_space=pltpu.VMEM), pl.BlockSpec(memory_space=pltpu.HBM)
    last = jax.ShapeDtypeStruct((shard, width), key_matrix.dtype)
    return pl.pallas_call(
        functools.partial(base_kernel, count + 2),
        name="base_products",
        in_specs=[inside] * (count + 1) + [outside] * 3,
        out_specs=[inside] * 4,
        scratch_shapes=[
            pltpu.VMEM((count, shard, width), key_matrix.dtype),
            pltpu.VMEM((count, shard, width), key_matrix.dtype),
            pltpu.SemaphoreType.DMA((2, count + 1)),
        ],
        out_shape=[
            jax.ShapeDtypeStruct((rows, 2 * width), jnp.float32),
            last,
            last,
            jax.ShapeDtypeStruct(mean.shape, mean.dtype),
        ],
        compiler_params=params(16),
        cost_estimate=cost(4 * count * rows * shard * width, count * (4 * shard * width + 2 * rows * shard)),
    )(*pieces, so_far, pinned(key_matrix), pinned(value_matrix), pinned(mean))


def last_kernel(count, total, *refs):
    sources, (keys, values, base_ref, out_ref, piece_ref, sem) = refs[:count], refs[count:]
    width = keys.shape[1]
    place = lax.axis_index("tp")
    outer = (place == 0) | (place == total - 1)
    for n, source in enumerate(sources):

        @pl.when(True if count == 1 else outer == (n == count - 1))
        def _():
            copy = pltpu.make_async_copy(source, piece_ref, sem)
            copy.start()
            copy.wait()

    for half, weights in enumerate((keys, values)):
        here = slice(half * width, (half + 1) * width)
        product = jnp.dot(piece_ref[...], weights[...], preferred_element_type=jnp.float32)
        out_ref[:, here] = base_ref[:, here] + product


def last_product(late, total, keys, values, base):
    inside, outside = pl.BlockSpec(memory_space=pltpu.VMEM), pl.BlockSpec(memory_space=pltpu.HBM)
    return pl.pallas_call(
        functools.partial(last_kernel, len(late), total),
        name="last_product",
        in_specs=[outside] * len(late) + [inside] * 3,
        out_specs=inside,
        out_shape=jax.ShapeDtypeStruct(base.shape, base.dtype),
        scratch_shapes=[pltpu.VMEM(late[0].shape, late[0].dtype), pltpu.SemaphoreType.DMA],
        compiler_params=params(8),
        cost_estimate=cost(2 * late[0].size * base.shape[1], 4 * keys.size),
    )(*late, keys, values, base)


def finish_kernel(base_ref, back_ref, pick_ref, query_ref, lse_ref, mean_ref, *refs):
    new_key_ref, new_value_ref, context_hbm, context_ref, sems = refs
    rows, wide = query_ref.shape
    width = new_key_ref.shape[1]
    heads = wide // HEAD_SIZE
    groups = width // HEAD_SIZE
    each = heads // groups
    inverse_root = HEAD_SIZE ** (-0.5)
    delta = jnp.dot(pick_ref[...], back_ref[...], preferred_element_type=jnp.float32)
    base = (base_ref[...] + delta).astype(jnp.bfloat16)
    new_key_ref[...] = base[:, :width]
    new_value_ref[...] = base[:, width:]
    keys, values = base[:, :width].astype(jnp.float32), base[:, width:].astype(jnp.float32)
    column = iota((rows, LANES), 1)
    own = jnp.zeros((rows, LANES), jnp.float32)
    for h in range(heads):
        k = h // each
        query = query_ref[:, h * HEAD_SIZE : (h + 1) * HEAD_SIZE].astype(jnp.float32)
        score = jnp.sum(query * keys[:, k * HEAD_SIZE : (k + 1) * HEAD_SIZE], axis=1, keepdims=True)
        own = jnp.where(column == h, score * inverse_root, own)
    share = 1.0 / (1.0 + jnp.exp(lse_ref[...] - own))
    for k in range(groups):
        for h in range(k * each, (k + 1) * each):
            mean = mean_ref[:, h * HEAD_SIZE : (h + 1) * HEAD_SIZE]
            mixed = mean + share[:, h : h + 1] * (values[:, k * HEAD_SIZE : (k + 1) * HEAD_SIZE] - mean)
            context_ref[:, h * HEAD_SIZE : (h + 1) * HEAD_SIZE] = mixed.astype(jnp.bfloat16)
        part = pl.ds(k * each * HEAD_SIZE, each * HEAD_SIZE)
        pltpu.make_async_copy(context_ref.at[:, part], context_hbm.at[:, part], sems.at[k]).start()
    for k in range(groups):
        part = pl.ds(k * each * HEAD_SIZE, each * HEAD_SIZE)
        pltpu.make_async_copy(context_ref.at[:, part], context_hbm.at[:, part], sems.at[k]).wait()


def finish(base, back, pick, queries, lse, mean):
    rows, wide = queries.shape
    width = base.shape[1] // 2
    inside, outside = pl.BlockSpec(memory_space=pltpu.VMEM), pl.BlockSpec(memory_space=pltpu.HBM)
    return pl.pallas_call(
        finish_kernel,
        name="finish_rows",
        in_specs=[inside] * 6,
        out_specs=[inside, inside, outside],
        out_shape=(
            jax.ShapeDtypeStruct((rows, width), jnp.bfloat16),
            jax.ShapeDtypeStruct((rows, width), jnp.bfloat16),
            jax.ShapeDtypeStruct((rows, wide), jnp.bfloat16),
        ),
        scratch_shapes=[
            pltpu.VMEM((rows, wide), jnp.bfloat16),
            pltpu.SemaphoreType.DMA((width // HEAD_SIZE,)),
        ],
        compiler_params=params(8),
        cost_estimate=cost(4 * rows * wide, 10 * rows * wide),
    )(base, back, pick, queries, lse, mean)


def swap(x, mask, size):
    return lax.ppermute(x, "tp", [(i, i ^ mask) for i in range(size)])


def turn(x, shift, size):
    return lax.ppermute(x, "tp", [(i, (i + shift) % size) for i in range(size)])


def others(x, size):
    return [turn(x, shift, size) for shift in range(1, size)]


def shards(
    hidden_in,
    queries,
    cache_keys,
    cached_value_rows,
    cache_lengths,
    base_key_matrix,
    base_value_matrix,
    shrink_weights,
    pooled_up_weights,
    block_owner,
    block_slot,
):
    rows_here, shard_width = hidden_in.shape
    replicas = lax.axis_size("rep")
    parts = lax.axis_size("tp")
    blocks_here = rows_here // BLK
    capacity = max(2, (2 * blocks_here + replicas - 1) // replicas)

    def all_to_all(x):
        kept = x.shape
        x = x.reshape(replicas, kept[0] // replicas, kept[1])
        return lax.all_to_all(x, "rep", split_axis=0, concat_axis=0, tiled=True).reshape(kept)

    outgoing, pick = pack(block_owner, block_slot, hidden_in, replicas, capacity)
    arrived = all_to_all(outgoing)

    if parts == 4:
        one = swap(hidden_in, 1, parts)
        two = swap(hidden_in, 2, parts)
    mean, lse, shrink_here = cached_attention(cache_lengths, queries, cache_keys, cached_value_rows, shrink_weights)
    arrived, lse = lax.optimization_barrier((arrived, lse))
    partial_rows, sent, flags = shrink(arrived, shrink_here)
    matrices = (base_key_matrix, base_value_matrix)
    partial_rows, own_piece = lax.optimization_barrier((partial_rows, hidden_in))
    base, up_here = own_product(own_piece, parts, *matrices, pooled_up_weights)
    if parts == 4:
        received = swap(sent, 1, parts)
        received, base = lax.optimization_barrier((received, base))
        paired = partial_rows + received.astype(jnp.float32)
        sums = [paired, swap(paired.astype(jnp.bfloat16), 2, parts)]
        one, two, again, _ = lax.optimization_barrier((one, two, hidden_in, paired))
        outer = lax.ppermute(two, "tp", [(1, 0), (2, 3)])
        inner = lax.ppermute(again, "tp", [(1, 2), (2, 1)])
        between, late = [one, two], [inner, outer]
    else:
        sums = [partial_rows] + others(sent, parts)
        pieces = others(hidden_in, parts)
        between, late = pieces[:-1], pieces[-1:]
    deltas = expand(sums, flags, up_here)
    back = all_to_all(deltas)
    deltas, *between = lax.optimization_barrier((deltas, *between))
    base, *last, mean = base_products(between, base, *matrices, mean)
    owner = owner_of(lax.axis_index("tp"), 1, parts)
    key_rows = lax.dynamic_slice_in_dim(base_key_matrix, owner * shard_width, shard_width, 0)
    more = jnp.dot(between[0], key_rows, preferred_element_type=jnp.float32)
    base = base + jnp.concatenate([more, jnp.zeros_like(more)], axis=1)
    base = last_product(late, parts, *last, base)
    return finish(base, back, pick, queries, lse, mean)


def solution(mesh):
    return jax.shard_map(
        shards,
        mesh=mesh,
        in_specs=(
            P("rep", "tp"),
            P("rep", "tp"),
            P("rep", None, "tp"),
            P("rep", None, "tp"),
            P("rep"),
            P(None, "tp"),
            P(None, "tp"),
            P("rep", "tp", None),
            P("rep", None, None, "tp"),
            P("rep", None),
            P("rep"),
        ),
        out_specs=(P("rep", "tp"), P("rep", "tp"), P("rep", "tp")),
        check_vma=False,
    )
```

```python
import functools

import jax
import jax.numpy as jnp
from jax import lax
from jax.experimental import pallas as pl
from jax.experimental.pallas import tpu as pltpu
from jax.sharding import PartitionSpec as P

HEAD_SIZE = 128
BLK = 4
LANES = 128
MIB = 1 << 20

adapter_scale = 0.5
masked_score = -1e30


def params(mib):
    return pltpu.CompilerParams(vmem_limit_bytes=mib * MIB)


def cost(flops, moved, exps=0):
    return pl.CostEstimate(flops=flops, bytes_accessed=moved, transcendentals=exps)


def pinned(x):
    return pltpu.with_memory_space_constraint(x, pltpu.HBM)


def iota(shape, dim):
    return lax.broadcasted_iota(jnp.int32, shape, dim)


def pack_kernel(capacity, owner_ref, slot_ref, hidden_ref, out_hbm, pick_hbm, out_ref, pick_ref, sems):
    blocks = owner_ref.shape[0]
    rows, width = hidden_ref.shape
    places = out_ref.shape[0]
    square = (blocks, blocks)
    down, across = iota(square, 0), iota(square, 1)
    owner_across = jnp.zeros((1, blocks), jnp.int32)
    owner_down = jnp.zeros((blocks, 1), jnp.int32)
    row_slot = jnp.zeros((rows, 1), jnp.int32)
    for b in range(blocks):
        owner_across = jnp.where(iota((1, blocks), 1) == b, owner_ref[b], owner_across)
        owner_down = jnp.where(iota((blocks, 1), 0) == b, owner_ref[b], owner_down)
        row_slot = jnp.where(iota((rows, 1), 0) // BLK == b, slot_ref[b], row_slot)
    same = (owner_down == owner_across) & (across < down)
    rank = jnp.sum(jnp.where(same, 1.0, 0.0), axis=1, keepdims=True)
    target = owner_down.astype(jnp.float32) * capacity + rank
    spread = iota((blocks, rows), 0) == iota((blocks, rows), 1) // BLK
    row_target = jnp.sum(jnp.where(spread, jnp.broadcast_to(target, (blocks, rows)), 0.0), axis=0, keepdims=True)
    row_target = row_target.astype(jnp.int32) * BLK + iota((1, rows), 1) % BLK
    pick = jnp.where(iota((places, rows), 0) == row_target, 1.0, 0.0).astype(jnp.bfloat16)
    flags = jnp.where(iota((rows, LANES), 1) == row_slot, 1.0, 0.0).astype(jnp.bfloat16)
    sent = []
    part = places // 2
    for n in range(2):
        here = slice(n * part, (n + 1) * part)
        out_ref[here, :width] = jnp.dot(pick[here], hidden_ref[...], preferred_element_type=jnp.float32).astype(jnp.bfloat16)
        out_ref[here, width:] = jnp.dot(pick[here], flags, preferred_element_type=jnp.float32).astype(jnp.bfloat16)
        rows_there = pl.ds(n * part, part)
        sent.append(pltpu.make_async_copy(out_ref.at[rows_there], out_hbm.at[rows_there], sems.at[n]))
        sent[n].start()
    gather = iota((rows, blocks), 1) == iota((rows, blocks), 0) // BLK
    target = jnp.sum(jnp.where(iota(square, 0) == iota(square, 1), target, 0.0), axis=0, keepdims=True)
    target = jnp.sum(jnp.where(gather, target, 0.0), axis=1, keepdims=True)
    target = target.astype(jnp.int32) * BLK + iota((rows, 1), 0) % BLK
    pick_ref[...] = jnp.where(iota((rows, places), 1) == target, 1.0, 0.0).astype(jnp.bfloat16)
    sent.append(pltpu.make_async_copy(pick_ref, pick_hbm, sems.at[2]))
    sent[-1].start()
    for copy in sent:
        copy.wait()


def pack(block_owner, block_slot, hidden, replicas, capacity):
    rows, width = hidden.shape
    places = replicas * capacity * BLK
    scalars = pl.BlockSpec(memory_space=pltpu.SMEM)
    outside = pl.BlockSpec(memory_space=pltpu.HBM)
    return pl.pallas_call(
        functools.partial(pack_kernel, capacity),
        name="pack_rows",
        in_specs=[scalars, scalars, pl.BlockSpec(memory_space=pltpu.VMEM)],
        out_specs=[outside, outside],
        out_shape=(
            pltpu.HBM((places, width + LANES), jnp.bfloat16),
            pltpu.HBM((rows, places), jnp.bfloat16),
        ),
        scratch_shapes=[
            pltpu.VMEM((places, width + LANES), jnp.bfloat16),
            pltpu.VMEM((rows, places), jnp.bfloat16),
            pltpu.SemaphoreType.DMA((3,)),
        ],
        compiler_params=params(61),
        cost_estimate=cost(2 * places * rows * width, 2 * (places + rows) * width),
    )(block_owner[:, 0], block_slot, hidden)


def shrink_kernel(rows_ref, shrink_ref, out_ref, sent_ref, flag_ref):
    pool, width, rank = shrink_ref.shape
    rows = rows_ref[:, :width]
    flag_ref[...] = rows_ref[:, width:]
    total = jnp.zeros(out_ref.shape, jnp.float32)
    for a in range(pool):
        part = jnp.dot(rows, shrink_ref[a], preferred_element_type=jnp.float32)
        total += part * rows_ref[:, width + a : width + a + 1].astype(jnp.float32)
    out_ref[...] = total
    sent_ref[...] = total.astype(jnp.bfloat16)


def shrink(arrived, weights):
    places = arrived.shape[0]
    pool, width, rank = weights.shape
    return pl.pallas_call(
        shrink_kernel,
        name="shrink_rows",
        out_shape=(
            jax.ShapeDtypeStruct((places, rank), jnp.float32),
            jax.ShapeDtypeStruct((places, rank), jnp.bfloat16),
            jax.ShapeDtypeStruct((places, LANES), jnp.bfloat16),
        ),
        compiler_params=params(8),
        cost_estimate=cost(2 * places * width * rank * pool, 2 * (places * width + weights.size)),
    )(arrived, weights)


def expand_kernel(count, *refs):
    parts, flag_ref, up_ref, out_ref = refs[:count], *refs[count:]
    pool, halves, rank, width = up_ref.shape
    total = parts[0][...].astype(jnp.float32)
    for part in parts[1:]:
        total += part[...].astype(jnp.float32)
    shrunk = total.astype(jnp.bfloat16)
    mine = [shrunk * flag_ref[:, a : a + 1] for a in range(pool)]
    side = iota(shrunk.shape, 1) // rank
    wide = [
        jnp.concatenate([jnp.where(side == half, x, jnp.zeros_like(x)) for x in mine], axis=1) for half in range(halves)
    ]
    table = up_ref[...].reshape(pool * halves * rank, width)
    for half in range(halves):
        product = jnp.dot(wide[half], table, preferred_element_type=jnp.float32)
        out_ref[:, half * width : (half + 1) * width] = (adapter_scale * product).astype(jnp.bfloat16)


def expand(parts, flags, up):
    places = parts[0].shape[0]
    pool, halves, rank, width = up.shape
    return pl.pallas_call(
        functools.partial(expand_kernel, len(parts)),
        name="expand_rows",
        out_shape=jax.ShapeDtypeStruct((places, halves * width), jnp.bfloat16),
        compiler_params=params(8),
        cost_estimate=cost(2 * places * up.size, 2 * up.size + 2 * places * halves * width),
    )(*parts, flags, up)


def cached_kernel(heads, group, length_hbm, query_hbm, key_hbm, value_hbm, shrink_hbm, *refs):
    groups = key_hbm.shape[2] // HEAD_SIZE
    mean_hbm, lse_ref, shrink_ref, length_ref, query_ref, keys, values, mean_ref, wide_q, wide_o, sems, more = refs
    rows, window, width = keys.shape
    each = heads // groups
    packed = LANES // heads
    inverse_root = HEAD_SIZE ** (-0.5)

    def copies(i):
        here = pl.ds(i * group, group)
        return (
            pltpu.make_async_copy(key_hbm.at[here], keys.at[here], sems.at[0, i]),
            pltpu.make_async_copy(value_hbm.at[here], values.at[here], sems.at[1, i]),
        )

    ahead = 2
    for i in range(ahead):
        for copy in copies(i):
            copy.start()
    small = [(length_hbm, length_ref), (query_hbm, query_ref), (shrink_hbm, shrink_ref)]
    small = [pltpu.make_async_copy(a, b, more.at[n]) for n, (a, b) in enumerate(small)]
    for copy in small:
        copy.start()
    wide_q[...] = jnp.zeros_like(wide_q)
    lane = iota((window, LANES), 1) // heads
    position = iota((window, LANES), 0)
    sublane = iota((packed, LANES), 0)

    small[0].wait()
    small[1].wait()

    def finished(i):
        here = pl.ds(pl.multiple_of(i * group, group), group)
        return pltpu.make_async_copy(mean_ref.at[here], mean_hbm.at[here], sems.at[2, i])

    def step(i, carry):
        start = pl.multiple_of(i * group, group)
        for h in range(heads):
            part = query_ref[pl.ds(start, group), h * HEAD_SIZE : (h + 1) * HEAD_SIZE]
            wide_q[h // each, pl.ds(h, group, stride=heads), :] = part.astype(jnp.float32)
        key_copy, value_copy = copies(i)
        key_copy.wait()

        @pl.when(i + ahead < rows // group)
        def _():
            for copy in copies(i + ahead):
                copy.start()

        all_weights = []
        for first in range(0, group, packed):
            here = pl.ds(first * heads, LANES)
            query = jnp.concatenate([wide_q[k, here, :] for k in range(groups)], axis=1).astype(jnp.bfloat16)
            block = keys[pl.ds(start + first, packed)].reshape(packed * window, width)
            product = lax.dot_general(block, query, (((1,), (1,)), ((), ())), preferred_element_type=jnp.float32)
            scores = jnp.zeros((window, LANES), jnp.float32)
            limit = jnp.zeros((1, LANES), jnp.int32)
            for r in range(packed):
                scores = jnp.where(lane == r, product[r * window : (r + 1) * window], scores)
                limit = jnp.where(lane[:1] == r, length_ref[start + first + r], limit)
            scores = jnp.where(position < limit, scores * inverse_root, masked_score)
            highest = jnp.max(scores, axis=0, keepdims=True)
            terms = jnp.exp(scores - highest)
            total = jnp.sum(terms, axis=0, keepdims=True)
            all_weights.append(jnp.transpose(terms * (1.0 / total)).astype(jnp.bfloat16))
            logs = jnp.broadcast_to(highest + jnp.log(total), (packed, LANES))
            spread = logs
            for r in range(1, packed):
                spread = jnp.where(sublane == r, pltpu.roll(logs, LANES - r * heads, 1), spread)
            lse_ref[pl.ds(start + first, packed), :] = spread
        value_copy.wait()
        for r in range(0, group, 2):
            weights = all_weights[r // packed][(r % packed) * heads : (r % packed + 2) * heads]
            upper = iota(weights.shape, 0) < heads
            zero = jnp.zeros_like(weights)
            weights = jnp.concatenate([jnp.where(upper, weights, zero), jnp.where(upper, zero, weights)], axis=1)
            block = values[pl.ds(start + r, 2)].reshape(2 * window, width)
            mixed = jnp.dot(weights, block, preferred_element_type=jnp.float32)
            for j in range(2):
                for k in range(groups):
                    mine = pl.ds((r + j) * heads + k * each, each)
                    top = j * heads + k * each
                    wide_o[mine, :] = mixed[top : top + each, k * HEAD_SIZE : (k + 1) * HEAD_SIZE]
        for h in range(heads):
            mean_ref[pl.ds(start, group), h * HEAD_SIZE : (h + 1) * HEAD_SIZE] = wide_o[pl.ds(h, group, stride=heads), :]
        finished(i).start()
        return carry

    lax.fori_loop(0, rows // group, step, 0)
    for i in range(rows // group):
        finished(i).wait()
    small[2].wait()


def cached_attention(lengths, queries, keys, values, weights):
    rows, window, width = keys.shape
    wide = queries.shape[1]
    heads = wide // HEAD_SIZE
    group = max(16, LANES // heads)
    groups = width // HEAD_SIZE
    inside, outside = pl.BlockSpec(memory_space=pltpu.VMEM), pl.BlockSpec(memory_space=pltpu.HBM)
    return pl.pallas_call(
        functools.partial(cached_kernel, heads, group),
        name="cached_attention",
        in_specs=[outside] * 5,
        out_specs=[outside, inside, inside],
        scratch_shapes=[
            pltpu.SMEM(lengths.shape, lengths.dtype),
            pltpu.VMEM(queries.shape, queries.dtype),
            pltpu.VMEM(keys.shape, keys.dtype),
            pltpu.VMEM(values.shape, values.dtype),
            pltpu.VMEM((rows, wide), jnp.float32),
            pltpu.VMEM((groups, group * heads, HEAD_SIZE), jnp.float32),
            pltpu.VMEM((group * heads, HEAD_SIZE), jnp.float32),
            pltpu.SemaphoreType.DMA((3, rows // group)),
            pltpu.SemaphoreType.DMA((3,)),
        ],
        out_shape=[
            pltpu.HBM((rows, wide), jnp.float32),
            jax.ShapeDtypeStruct((rows, LANES), jnp.float32),
            jax.ShapeDtypeStruct(weights.shape, weights.dtype),
        ],
        compiler_params=params(20),
        cost_estimate=cost(4 * rows * heads * window * width, 4 * keys.size + 6 * rows * wide, rows * heads * window),
    )(*(pinned(x) for x in (lengths, queries, keys, values, weights)))


def owner_of(place, p, parts):
    return place ^ p if parts == 4 else lax.rem(place + parts - p, parts)


def early_kernel(count, total, *refs):
    pieces, (key_hbm, value_hbm, up_hbm, out_ref, up_ref, keys, values, sems) = refs[:count], refs[count:]
    shard, width = keys.shape[1:]
    place = lax.axis_index("tp")
    copies = []
    for p in range(count):
        rows = pl.ds(pl.multiple_of(owner_of(place, p, total) * shard, shard), shard)
        copies.append(pltpu.make_async_copy(key_hbm.at[rows], keys.at[p], sems.at[0, p]))
        copies.append(pltpu.make_async_copy(value_hbm.at[rows], values.at[p], sems.at[1, p]))
    copies.append(pltpu.make_async_copy(up_hbm, up_ref, sems.at[0, count]))
    for copy in copies:
        copy.start()
    for p in range(count):
        for half, weights in enumerate((keys, values)):
            here = slice(half * width, (half + 1) * width)
            copies[2 * p + half].wait()
            product = jnp.dot(pieces[p][...], weights[p], preferred_element_type=jnp.float32)
            out_ref[:, here] = out_ref[:, here] + product if p else product
    copies[-1].wait()


def early_products(pieces, total, key_matrix, value_matrix, up):
    rows, shard = pieces[0].shape
    width = key_matrix.shape[1]
    count = len(pieces)
    inside, outside = pl.BlockSpec(memory_space=pltpu.VMEM), pl.BlockSpec(memory_space=pltpu.HBM)
    return pl.pallas_call(
        functools.partial(early_kernel, count, total),
        name="early_products",
        in_specs=[inside] * count + [outside, outside, outside],
        out_specs=[inside, inside],
        out_shape=[jax.ShapeDtypeStruct((rows, 2 * width), jnp.float32), jax.ShapeDtypeStruct(up.shape, up.dtype)],
        scratch_shapes=[pltpu.VMEM((count, shard, width), key_matrix.dtype)] * 2
        + [pltpu.SemaphoreType.DMA((2, count + 1))],
        compiler_params=params(12),
        cost_estimate=cost(4 * count * rows * shard * width, 4 * count * shard * width),
    )(*pieces, pinned(key_matrix), pinned(value_matrix), pinned(up))


def base_kernel(first, total, *refs):
    count = total - 1 - first
    pieces, refs = refs[:count], refs[count:]
    so_far, key_hbm, value_hbm, mean_hbm, out_ref, last_keys, last_values, mean_ref, keys, values, sems = refs
    shard, width = last_keys.shape
    place = lax.axis_index("tp")

    def copies(p):
        rows = pl.ds(pl.multiple_of(owner_of(place, p + first, total) * shard, shard), shard)
        key_to, value_to = (last_keys, last_values) if p == count else (keys.at[p], values.at[p])
        key_copy = pltpu.make_async_copy(key_hbm.at[rows], key_to, sems.at[0, p]) if p > 0 else None
        return key_copy, pltpu.make_async_copy(value_hbm.at[rows], value_to, sems.at[1, p])

    everything = [copy for p in range(count + 1) for copy in copies(p) if copy is not None]
    everything.append(pltpu.make_async_copy(mean_hbm, mean_ref, sems.at[0, 0]))
    for copy in everything:
        copy.start()
    out_ref[...] = so_far[...]
    for p in range(count):
        for half, (copy, weights) in enumerate(zip(copies(p), (keys, values))):
            if copy is None:
                continue
            here = slice(half * width, (half + 1) * width)
            copy.wait()
            out_ref[:, here] += jnp.dot(pieces[p][...], weights[p], preferred_element_type=jnp.float32)
    for copy in everything[-3:]:
        copy.wait()


def base_products(pieces, total, so_far, key_matrix, value_matrix, mean):
    rows, shard = pieces[0].shape
    width = key_matrix.shape[1]
    count = len(pieces)
    inside, outside = pl.BlockSpec(memory_space=pltpu.VMEM), pl.BlockSpec(memory_space=pltpu.HBM)
    last = jax.ShapeDtypeStruct((shard, width), key_matrix.dtype)
    return pl.pallas_call(
        functools.partial(base_kernel, total - 1 - count, total),
        name="base_products",
        in_specs=[inside] * (count + 1) + [outside] * 3,
        out_specs=[inside] * 4,
        scratch_shapes=[
            pltpu.VMEM((count, shard, width), key_matrix.dtype),
            pltpu.VMEM((count, shard, width), key_matrix.dtype),
            pltpu.SemaphoreType.DMA((2, count + 1)),
        ],
        out_shape=[
            jax.ShapeDtypeStruct((rows, 2 * width), jnp.float32),
            last,
            last,
            jax.ShapeDtypeStruct(mean.shape, mean.dtype),
        ],
        compiler_params=params(16),
        cost_estimate=cost(4 * count * rows * shard * width, count * (4 * shard * width + 2 * rows * shard)),
    )(*pieces, so_far, pinned(key_matrix), pinned(value_matrix), pinned(mean))


def last_kernel(piece_ref, keys, values, base_ref, out_ref):
    width = keys.shape[1]
    for half, weights in enumerate((keys, values)):
        here = slice(half * width, (half + 1) * width)
        product = jnp.dot(piece_ref[...], weights[...], preferred_element_type=jnp.float32)
        out_ref[:, here] = base_ref[:, here] + product


def last_product(late, keys, values, base):
    return pl.pallas_call(
        last_kernel,
        name="last_product",
        out_shape=jax.ShapeDtypeStruct(base.shape, base.dtype),
        compiler_params=params(8),
        cost_estimate=cost(2 * late.size * base.shape[1], 4 * keys.size),
    )(late, keys, values, base)


def finish_kernel(base_ref, back_ref, pick_ref, query_ref, lse_ref, mean_ref, *refs):
    new_key_hbm, new_value_hbm, context_hbm, new_ref, context_ref, sems = refs
    rows, wide = query_ref.shape
    width = new_ref.shape[2]
    heads = wide // HEAD_SIZE
    groups = width // HEAD_SIZE
    each = heads // groups
    inverse_root = HEAD_SIZE ** (-0.5)
    delta = jnp.dot(pick_ref[...], back_ref[...], preferred_element_type=jnp.float32)
    base = (base_ref[...] + delta).astype(jnp.bfloat16)
    sent = []
    for half, target in enumerate((new_key_hbm, new_value_hbm)):
        new_ref[half] = base[:, half * width : (half + 1) * width]
        sent.append(pltpu.make_async_copy(new_ref.at[half], target, sems.at[groups + half]))
        sent[half].start()
    keys, values = base[:, :width].astype(jnp.float32), base[:, width:].astype(jnp.float32)
    column = iota((rows, LANES), 1)
    own = jnp.zeros((rows, LANES), jnp.float32)
    for h in range(heads):
        k = h // each
        query = query_ref[:, h * HEAD_SIZE : (h + 1) * HEAD_SIZE].astype(jnp.float32)
        score = jnp.sum(query * keys[:, k * HEAD_SIZE : (k + 1) * HEAD_SIZE], axis=1, keepdims=True)
        own = jnp.where(column == h, score * inverse_root, own)
    share = 1.0 / (1.0 + jnp.exp(lse_ref[...] - own))
    for k in range(groups):
        for h in range(k * each, (k + 1) * each):
            mean = mean_ref[:, h * HEAD_SIZE : (h + 1) * HEAD_SIZE]
            mixed = mean + share[:, h : h + 1] * (values[:, k * HEAD_SIZE : (k + 1) * HEAD_SIZE] - mean)
            context_ref[:, h * HEAD_SIZE : (h + 1) * HEAD_SIZE] = mixed.astype(jnp.bfloat16)
        part = pl.ds(k * each * HEAD_SIZE, each * HEAD_SIZE)
        sent.append(pltpu.make_async_copy(context_ref.at[:, part], context_hbm.at[:, part], sems.at[k]))
        sent[-1].start()
    for copy in sent:
        copy.wait()


def finish(base, back, pick, queries, lse, mean):
    rows, wide = queries.shape
    width = base.shape[1] // 2
    inside, outside = pl.BlockSpec(memory_space=pltpu.VMEM), pl.BlockSpec(memory_space=pltpu.HBM)
    return pl.pallas_call(
        finish_kernel,
        name="finish_rows",
        in_specs=[inside] * 6,
        out_specs=[outside] * 3,
        out_shape=(
            jax.ShapeDtypeStruct((rows, width), jnp.bfloat16),
            jax.ShapeDtypeStruct((rows, width), jnp.bfloat16),
            jax.ShapeDtypeStruct((rows, wide), jnp.bfloat16),
        ),
        scratch_shapes=[
            pltpu.VMEM((2, rows, width), jnp.bfloat16),
            pltpu.VMEM((rows, wide), jnp.bfloat16),
            pltpu.SemaphoreType.DMA((width // HEAD_SIZE + 2,)),
        ],
        compiler_params=params(8),
        cost_estimate=cost(4 * rows * wide, 10 * rows * wide),
    )(base, back, pick, queries, lse, mean)


def swap(x, mask, size):
    return lax.ppermute(x, "tp", [(i, i ^ mask) for i in range(size)])


def turn(x, shift, size):
    return lax.ppermute(x, "tp", [(i, (i + shift) % size) for i in range(size)])


def others(x, size):
    return [turn(x, shift, size) for shift in range(1, size)]


def shards(
    hidden_in,
    queries,
    cache_keys,
    cached_value_rows,
    cache_lengths,
    base_key_matrix,
    base_value_matrix,
    shrink_weights,
    pooled_up_weights,
    block_owner,
    block_slot,
):
    rows_here, shard_width = hidden_in.shape
    replicas = lax.axis_size("rep")
    parts = lax.axis_size("tp")
    blocks_here = rows_here // BLK
    capacity = max(2, (2 * blocks_here + replicas - 1) // replicas)

    def all_to_all(x):
        kept = x.shape
        x = x.reshape(replicas, kept[0] // replicas, kept[1])
        return lax.all_to_all(x, "rep", split_axis=0, concat_axis=0, tiled=True).reshape(kept)

    outgoing, pick = pack(block_owner, block_slot, hidden_in, replicas, capacity)
    arrived = all_to_all(outgoing)

    if parts == 4:
        one = swap(hidden_in, 1, parts)
        two = swap(hidden_in, 2, parts)
    mean, lse, shrink_here = cached_attention(cache_lengths, queries, cache_keys, cached_value_rows, shrink_weights)
    arrived, lse = lax.optimization_barrier((arrived, lse))
    partial_rows, sent, flags = shrink(arrived, shrink_here)
    matrices = (base_key_matrix, base_value_matrix)
    if parts == 4:
        pieces = [hidden_in, one]
        received = swap(sent, 1, parts)
    else:
        pieces = [hidden_in] + others(hidden_in, parts)
    early = 1
    sent, *first = lax.optimization_barrier((sent, *pieces[:early]))
    base, up_here = early_products(first, parts, *matrices, pooled_up_weights)
    if parts == 4:
        received, base = lax.optimization_barrier((received, base))
        paired = partial_rows + received.astype(jnp.float32)
        sums = [paired, swap(paired.astype(jnp.bfloat16), 2, parts)]
        one, two, _ = lax.optimization_barrier((one, two, paired))
        pieces = [hidden_in, one, two, swap(two, 1, parts)]
    else:
        sums = [partial_rows] + others(sent, parts)
    deltas = expand(sums, flags, up_here)
    back = all_to_all(deltas)
    deltas, *between = lax.optimization_barrier((deltas, *pieces[early:-1]))
    base, *last, mean = base_products(between, parts, base, *matrices, mean)
    owner = owner_of(lax.axis_index("tp"), early, parts)
    key_rows = lax.dynamic_slice_in_dim(base_key_matrix, owner * shard_width, shard_width, 0)
    more = jnp.dot(between[0], key_rows, preferred_element_type=jnp.float32)
    base = base + jnp.concatenate([more, jnp.zeros_like(more)], axis=1)
    base = last_product(pieces[-1], *last, base)
    return finish(base, back, pick, queries, lse, mean)


def solution(mesh):
    return jax.shard_map(
        shards,
        mesh=mesh,
        in_specs=(
            P("rep", "tp"),
            P("rep", "tp"),
            P("rep", None, "tp"),
            P("rep", None, "tp"),
            P("rep"),
            P(None, "tp"),
            P(None, "tp"),
            P("rep", "tp", None),
            P("rep", None, None, "tp"),
            P("rep", None),
            P("rep"),
        ),
        out_specs=(P("rep", "tp"), P("rep", "tp"), P("rep", "tp")),
        check_vma=False,
    )
```

```python
import functools

import jax
import jax.numpy as jnp
from jax import lax
from jax.experimental import pallas as pl
from jax.experimental.pallas import tpu as pltpu
from jax.sharding import PartitionSpec as P

HEAD_SIZE = 128
BLK = 4
LANES = 128
MIB = 1 << 20

adapter_scale = 0.5
masked_score = -1e30


def params(mib):
    return pltpu.CompilerParams(vmem_limit_bytes=mib * MIB)


def cost(flops, moved, exps=0):
    return pl.CostEstimate(flops=flops, bytes_accessed=moved, transcendentals=exps)


def pinned(x):
    return pltpu.with_memory_space_constraint(x, pltpu.HBM)


def iota(shape, dim):
    return lax.broadcasted_iota(jnp.int32, shape, dim)


def pack_kernel(capacity, owner_ref, slot_ref, hidden_ref, out_hbm, pick_hbm, out_ref, pick_ref, sems):
    blocks = owner_ref.shape[0]
    rows, width = hidden_ref.shape
    places = out_ref.shape[0]
    square = (blocks, blocks)
    down, across = iota(square, 0), iota(square, 1)
    owner_across = jnp.zeros((1, blocks), jnp.int32)
    owner_down = jnp.zeros((blocks, 1), jnp.int32)
    row_slot = jnp.zeros((rows, 1), jnp.int32)
    for b in range(blocks):
        owner_across = jnp.where(iota((1, blocks), 1) == b, owner_ref[b], owner_across)
        owner_down = jnp.where(iota((blocks, 1), 0) == b, owner_ref[b], owner_down)
        row_slot = jnp.where(iota((rows, 1), 0) // BLK == b, slot_ref[b], row_slot)
    same = (owner_down == owner_across) & (across < down)
    rank = jnp.sum(jnp.where(same, 1.0, 0.0), axis=1, keepdims=True)
    target = owner_down.astype(jnp.float32) * capacity + rank
    spread = iota((blocks, rows), 0) == iota((blocks, rows), 1) // BLK
    row_target = jnp.sum(jnp.where(spread, jnp.broadcast_to(target, (blocks, rows)), 0.0), axis=0, keepdims=True)
    row_target = row_target.astype(jnp.int32) * BLK + iota((1, rows), 1) % BLK
    pick = jnp.where(iota((places, rows), 0) == row_target, 1.0, 0.0).astype(jnp.bfloat16)
    flags = jnp.where(iota((rows, LANES), 1) == row_slot, 1.0, 0.0).astype(jnp.bfloat16)
    sent = []
    part = places // 2
    for n in range(2):
        here = slice(n * part, (n + 1) * part)
        out_ref[here, :width] = jnp.dot(pick[here], hidden_ref[...], preferred_element_type=jnp.float32).astype(jnp.bfloat16)
        out_ref[here, width:] = jnp.dot(pick[here], flags, preferred_element_type=jnp.float32).astype(jnp.bfloat16)
        rows_there = pl.ds(n * part, part)
        sent.append(pltpu.make_async_copy(out_ref.at[rows_there], out_hbm.at[rows_there], sems.at[n]))
        sent[n].start()
    gather = iota((rows, blocks), 1) == iota((rows, blocks), 0) // BLK
    target = jnp.sum(jnp.where(iota(square, 0) == iota(square, 1), target, 0.0), axis=0, keepdims=True)
    target = jnp.sum(jnp.where(gather, target, 0.0), axis=1, keepdims=True)
    target = target.astype(jnp.int32) * BLK + iota((rows, 1), 0) % BLK
    pick_ref[...] = jnp.where(iota((rows, places), 1) == target, 1.0, 0.0).astype(jnp.bfloat16)
    sent.append(pltpu.make_async_copy(pick_ref, pick_hbm, sems.at[2]))
    sent[-1].start()
    for copy in sent:
        copy.wait()


def pack(block_owner, block_slot, hidden, replicas, capacity):
    rows, width = hidden.shape
    places = replicas * capacity * BLK
    scalars = pl.BlockSpec(memory_space=pltpu.SMEM)
    outside = pl.BlockSpec(memory_space=pltpu.HBM)
    return pl.pallas_call(
        functools.partial(pack_kernel, capacity),
        name="pack_rows",
        in_specs=[scalars, scalars, pl.BlockSpec(memory_space=pltpu.VMEM)],
        out_specs=[outside, outside],
        out_shape=(
            pltpu.HBM((places, width + LANES), jnp.bfloat16),
            pltpu.HBM((rows, places), jnp.bfloat16),
        ),
        scratch_shapes=[
            pltpu.VMEM((places, width + LANES), jnp.bfloat16),
            pltpu.VMEM((rows, places), jnp.bfloat16),
            pltpu.SemaphoreType.DMA((3,)),
        ],
        compiler_params=params(61),
        cost_estimate=cost(2 * places * rows * width, 2 * (places + rows) * width),
    )(block_owner[:, 0], block_slot, hidden)


def shrink_kernel(rows_ref, shrink_ref, out_ref, sent_ref, flag_ref):
    pool, width, rank = shrink_ref.shape
    rows = rows_ref[:, :width]
    flag_ref[...] = rows_ref[:, width:]
    total = jnp.zeros(out_ref.shape, jnp.float32)
    for a in range(pool):
        part = jnp.dot(rows, shrink_ref[a], preferred_element_type=jnp.float32)
        total += part * rows_ref[:, width + a : width + a + 1].astype(jnp.float32)
    out_ref[...] = total
    sent_ref[...] = total.astype(jnp.bfloat16)


def shrink(arrived, weights):
    places = arrived.shape[0]
    pool, width, rank = weights.shape
    return pl.pallas_call(
        shrink_kernel,
        name="shrink_rows",
        out_shape=(
            jax.ShapeDtypeStruct((places, rank), jnp.float32),
            jax.ShapeDtypeStruct((places, rank), jnp.bfloat16),
            jax.ShapeDtypeStruct((places, LANES), jnp.bfloat16),
        ),
        compiler_params=params(8),
        cost_estimate=cost(2 * places * width * rank * pool, 2 * (places * width + weights.size)),
    )(arrived, weights)


def expand_kernel(count, *refs):
    parts, flag_ref, up_ref, out_ref = refs[:count], *refs[count:]
    pool, halves, rank, width = up_ref.shape
    total = parts[0][...].astype(jnp.float32)
    for part in parts[1:]:
        total += part[...].astype(jnp.float32)
    shrunk = total.astype(jnp.bfloat16)
    mine = [shrunk * flag_ref[:, a : a + 1] for a in range(pool)]
    side = iota(shrunk.shape, 1) // rank
    wide = [
        jnp.concatenate([jnp.where(side == half, x, jnp.zeros_like(x)) for x in mine], axis=1) for half in range(halves)
    ]
    table = up_ref[...].reshape(pool * halves * rank, width)
    for half in range(halves):
        product = jnp.dot(wide[half], table, preferred_element_type=jnp.float32)
        out_ref[:, half * width : (half + 1) * width] = (adapter_scale * product).astype(jnp.bfloat16)


def expand(parts, flags, up):
    places = parts[0].shape[0]
    pool, halves, rank, width = up.shape
    return pl.pallas_call(
        functools.partial(expand_kernel, len(parts)),
        name="expand_rows",
        out_shape=jax.ShapeDtypeStruct((places, halves * width), jnp.bfloat16),
        compiler_params=params(8),
        cost_estimate=cost(2 * places * up.size, 2 * up.size + 2 * places * halves * width),
    )(*parts, flags, up)


def cached_kernel(heads, group, length_hbm, query_hbm, key_hbm, value_hbm, shrink_hbm, *refs):
    groups = key_hbm.shape[2] // HEAD_SIZE
    mean_hbm, lse_ref, shrink_ref, length_ref, query_ref, keys, values, mean_ref, wide_q, wide_o, sems, more = refs
    rows, window, width = keys.shape
    each = heads // groups
    packed = LANES // heads
    inverse_root = HEAD_SIZE ** (-0.5)

    def copies(i):
        here = pl.ds(i * group, group)
        return (
            pltpu.make_async_copy(key_hbm.at[here], keys.at[here], sems.at[0, i]),
            pltpu.make_async_copy(value_hbm.at[here], values.at[here], sems.at[1, i]),
        )

    ahead = 2
    for i in range(ahead):
        for copy in copies(i):
            copy.start()
    small = [(length_hbm, length_ref), (query_hbm, query_ref), (shrink_hbm, shrink_ref)]
    small = [pltpu.make_async_copy(a, b, more.at[n]) for n, (a, b) in enumerate(small)]
    for copy in small:
        copy.start()
    wide_q[...] = jnp.zeros_like(wide_q)
    lane = iota((window, LANES), 1) // heads
    position = iota((window, LANES), 0)
    sublane = iota((packed, LANES), 0)

    small[0].wait()
    small[1].wait()

    def finished(i):
        here = pl.ds(pl.multiple_of(i * group, group), group)
        return pltpu.make_async_copy(mean_ref.at[here], mean_hbm.at[here], sems.at[2, i])

    def step(i, carry):
        start = pl.multiple_of(i * group, group)
        for h in range(heads):
            part = query_ref[pl.ds(start, group), h * HEAD_SIZE : (h + 1) * HEAD_SIZE]
            wide_q[h // each, pl.ds(h, group, stride=heads), :] = part.astype(jnp.float32)
        key_copy, value_copy = copies(i)
        key_copy.wait()

        @pl.when(i + ahead < rows // group)
        def _():
            for copy in copies(i + ahead):
                copy.start()

        all_weights = []
        for first in range(0, group, packed):
            here = pl.ds(first * heads, LANES)
            query = jnp.concatenate([wide_q[k, here, :] for k in range(groups)], axis=1).astype(jnp.bfloat16)
            block = keys[pl.ds(start + first, packed)].reshape(packed * window, width)
            product = lax.dot_general(block, query, (((1,), (1,)), ((), ())), preferred_element_type=jnp.float32)
            scores = jnp.zeros((window, LANES), jnp.float32)
            limit = jnp.zeros((1, LANES), jnp.int32)
            for r in range(packed):
                scores = jnp.where(lane == r, product[r * window : (r + 1) * window], scores)
                limit = jnp.where(lane[:1] == r, length_ref[start + first + r], limit)
            scores = jnp.where(position < limit, scores * inverse_root, masked_score)
            highest = jnp.max(scores, axis=0, keepdims=True)
            terms = jnp.exp(scores - highest)
            total = jnp.sum(terms, axis=0, keepdims=True)
            all_weights.append(jnp.transpose(terms * (1.0 / total)).astype(jnp.bfloat16))
            logs = jnp.broadcast_to(highest + jnp.log(total), (packed, LANES))
            spread = logs
            for r in range(1, packed):
                spread = jnp.where(sublane == r, pltpu.roll(logs, LANES - r * heads, 1), spread)
            lse_ref[pl.ds(start + first, packed), :] = spread
        value_copy.wait()
        for r in range(0, group, 2):
            weights = all_weights[r // packed][(r % packed) * heads : (r % packed + 2) * heads]
            upper = iota(weights.shape, 0) < heads
            zero = jnp.zeros_like(weights)
            weights = jnp.concatenate([jnp.where(upper, weights, zero), jnp.where(upper, zero, weights)], axis=1)
            block = values[pl.ds(start + r, 2)].reshape(2 * window, width)
            mixed = jnp.dot(weights, block, preferred_element_type=jnp.float32)
            for j in range(2):
                for k in range(groups):
                    mine = pl.ds((r + j) * heads + k * each, each)
                    top = j * heads + k * each
                    wide_o[mine, :] = mixed[top : top + each, k * HEAD_SIZE : (k + 1) * HEAD_SIZE]
        for h in range(heads):
            mean_ref[pl.ds(start, group), h * HEAD_SIZE : (h + 1) * HEAD_SIZE] = wide_o[pl.ds(h, group, stride=heads), :]
        finished(i).start()
        return carry

    lax.fori_loop(0, rows // group, step, 0)
    for i in range(rows // group):
        finished(i).wait()
    small[2].wait()


def cached_attention(lengths, queries, keys, values, weights):
    rows, window, width = keys.shape
    wide = queries.shape[1]
    heads = wide // HEAD_SIZE
    group = max(16, LANES // heads)
    groups = width // HEAD_SIZE
    inside, outside = pl.BlockSpec(memory_space=pltpu.VMEM), pl.BlockSpec(memory_space=pltpu.HBM)
    return pl.pallas_call(
        functools.partial(cached_kernel, heads, group),
        name="cached_attention",
        in_specs=[outside] * 5,
        out_specs=[outside, inside, inside],
        scratch_shapes=[
            pltpu.SMEM(lengths.shape, lengths.dtype),
            pltpu.VMEM(queries.shape, queries.dtype),
            pltpu.VMEM(keys.shape, keys.dtype),
            pltpu.VMEM(values.shape, values.dtype),
            pltpu.VMEM((rows, wide), jnp.float32),
            pltpu.VMEM((groups, group * heads, HEAD_SIZE), jnp.float32),
            pltpu.VMEM((group * heads, HEAD_SIZE), jnp.float32),
            pltpu.SemaphoreType.DMA((3, rows // group)),
            pltpu.SemaphoreType.DMA((3,)),
        ],
        out_shape=[
            pltpu.HBM((rows, wide), jnp.float32),
            jax.ShapeDtypeStruct((rows, LANES), jnp.float32),
            jax.ShapeDtypeStruct(weights.shape, weights.dtype),
        ],
        compiler_params=params(20),
        cost_estimate=cost(4 * rows * heads * window * width, 4 * keys.size + 6 * rows * wide, rows * heads * window),
    )(*(pinned(x) for x in (lengths, queries, keys, values, weights)))


def owner_of(place, p, parts):
    return place ^ p if parts == 4 else lax.rem(place + parts - p, parts)


def early_kernel(count, total, *refs):
    pieces, (key_hbm, value_hbm, up_hbm, out_ref, up_ref, keys, values, sems) = refs[:count], refs[count:]
    shard, width = keys.shape[1:]
    place = lax.axis_index("tp")
    copies = []
    for p in range(count):
        rows = pl.ds(pl.multiple_of(owner_of(place, p, total) * shard, shard), shard)
        copies.append(pltpu.make_async_copy(key_hbm.at[rows], keys.at[p], sems.at[0, p]))
        copies.append(pltpu.make_async_copy(value_hbm.at[rows], values.at[p], sems.at[1, p]))
    copies.append(pltpu.make_async_copy(up_hbm, up_ref, sems.at[0, count]))
    for copy in copies:
        copy.start()
    for p in range(count):
        for half, weights in enumerate((keys, values)):
            here = slice(half * width, (half + 1) * width)
            copies[2 * p + half].wait()
            product = jnp.dot(pieces[p][...], weights[p], preferred_element_type=jnp.float32)
            out_ref[:, here] = out_ref[:, here] + product if p else product
    copies[-1].wait()


def early_products(pieces, total, key_matrix, value_matrix, up):
    rows, shard = pieces[0].shape
    width = key_matrix.shape[1]
    count = len(pieces)
    inside, outside = pl.BlockSpec(memory_space=pltpu.VMEM), pl.BlockSpec(memory_space=pltpu.HBM)
    return pl.pallas_call(
        functools.partial(early_kernel, count, total),
        name="early_products",
        in_specs=[inside] * count + [outside, outside, outside],
        out_specs=[inside, inside],
        out_shape=[jax.ShapeDtypeStruct((rows, 2 * width), jnp.float32), jax.ShapeDtypeStruct(up.shape, up.dtype)],
        scratch_shapes=[pltpu.VMEM((count, shard, width), key_matrix.dtype)] * 2
        + [pltpu.SemaphoreType.DMA((2, count + 1))],
        compiler_params=params(12),
        cost_estimate=cost(4 * count * rows * shard * width, 4 * count * shard * width),
    )(*pieces, pinned(key_matrix), pinned(value_matrix), pinned(up))


def base_kernel(first, total, *refs):
    count = total - 1 - first
    pieces, refs = refs[:count], refs[count:]
    so_far, key_hbm, value_hbm, mean_hbm, out_ref, last_keys, last_values, mean_ref, keys, values, sems = refs
    shard, width = last_keys.shape
    place = lax.axis_index("tp")

    def copies(p):
        rows = pl.ds(pl.multiple_of(owner_of(place, p + first, total) * shard, shard), shard)
        key_to, value_to = (last_keys, last_values) if p == count else (keys.at[p], values.at[p])
        key_copy = pltpu.make_async_copy(key_hbm.at[rows], key_to, sems.at[0, p]) if p > 0 else None
        return key_copy, pltpu.make_async_copy(value_hbm.at[rows], value_to, sems.at[1, p])

    everything = [copy for p in range(count + 1) for copy in copies(p) if copy is not None]
    everything.append(pltpu.make_async_copy(mean_hbm, mean_ref, sems.at[0, 0]))
    for copy in everything:
        copy.start()
    out_ref[...] = so_far[...]
    for p in range(count):
        for half, (copy, weights) in enumerate(zip(copies(p), (keys, values))):
            if copy is None:
                continue
            here = slice(half * width, (half + 1) * width)
            copy.wait()
            out_ref[:, here] += jnp.dot(pieces[p][...], weights[p], preferred_element_type=jnp.float32)
    for copy in everything[-3:]:
        copy.wait()


def base_products(pieces, total, so_far, key_matrix, value_matrix, mean):
    rows, shard = pieces[0].shape
    width = key_matrix.shape[1]
    count = len(pieces)
    inside, outside = pl.BlockSpec(memory_space=pltpu.VMEM), pl.BlockSpec(memory_space=pltpu.HBM)
    last = jax.ShapeDtypeStruct((shard, width), key_matrix.dtype)
    return pl.pallas_call(
        functools.partial(base_kernel, total - 1 - count, total),
        name="base_products",
        in_specs=[inside] * (count + 1) + [outside] * 3,
        out_specs=[inside] * 4,
        scratch_shapes=[
            pltpu.VMEM((count, shard, width), key_matrix.dtype),
            pltpu.VMEM((count, shard, width), key_matrix.dtype),
            pltpu.SemaphoreType.DMA((2, count + 1)),
        ],
        out_shape=[
            jax.ShapeDtypeStruct((rows, 2 * width), jnp.float32),
            last,
            last,
            jax.ShapeDtypeStruct(mean.shape, mean.dtype),
        ],
        compiler_params=params(16),
        cost_estimate=cost(4 * count * rows * shard * width, count * (4 * shard * width + 2 * rows * shard)),
    )(*pieces, so_far, pinned(key_matrix), pinned(value_matrix), pinned(mean))


def last_kernel(piece_ref, keys, values, base_ref, out_ref):
    width = keys.shape[1]
    for half, weights in enumerate((keys, values)):
        here = slice(half * width, (half + 1) * width)
        product = jnp.dot(piece_ref[...], weights[...], preferred_element_type=jnp.float32)
        out_ref[:, here] = base_ref[:, here] + product


def last_product(late, keys, values, base):
    return pl.pallas_call(
        last_kernel,
        name="last_product",
        out_shape=jax.ShapeDtypeStruct(base.shape, base.dtype),
        compiler_params=params(8),
        cost_estimate=cost(2 * late.size * base.shape[1], 4 * keys.size),
    )(late, keys, values, base)


def finish_kernel(base_ref, back_ref, pick_ref, query_ref, lse_ref, mean_ref, *refs):
    new_key_hbm, new_value_hbm, context_hbm, new_ref, context_ref, sems = refs
    rows, wide = query_ref.shape
    width = new_ref.shape[2]
    heads = wide // HEAD_SIZE
    groups = width // HEAD_SIZE
    each = heads // groups
    inverse_root = HEAD_SIZE ** (-0.5)
    delta = jnp.dot(pick_ref[...], back_ref[...], preferred_element_type=jnp.float32)
    base = (base_ref[...] + delta).astype(jnp.bfloat16)
    sent = []
    for half, target in enumerate((new_key_hbm, new_value_hbm)):
        new_ref[half] = base[:, half * width : (half + 1) * width]
        sent.append(pltpu.make_async_copy(new_ref.at[half], target, sems.at[groups + half]))
        sent[half].start()
    keys, values = base[:, :width].astype(jnp.float32), base[:, width:].astype(jnp.float32)
    column = iota((rows, LANES), 1)
    own = jnp.zeros((rows, LANES), jnp.float32)
    for h in range(heads):
        k = h // each
        query = query_ref[:, h * HEAD_SIZE : (h + 1) * HEAD_SIZE].astype(jnp.float32)
        score = jnp.sum(query * keys[:, k * HEAD_SIZE : (k + 1) * HEAD_SIZE], axis=1, keepdims=True)
        own = jnp.where(column == h, score * inverse_root, own)
    share = 1.0 / (1.0 + jnp.exp(lse_ref[...] - own))
    for k in range(groups):
        for h in range(k * each, (k + 1) * each):
            mean = mean_ref[:, h * HEAD_SIZE : (h + 1) * HEAD_SIZE]
            mixed = mean + share[:, h : h + 1] * (values[:, k * HEAD_SIZE : (k + 1) * HEAD_SIZE] - mean)
            context_ref[:, h * HEAD_SIZE : (h + 1) * HEAD_SIZE] = mixed.astype(jnp.bfloat16)
        part = pl.ds(k * each * HEAD_SIZE, each * HEAD_SIZE)
        sent.append(pltpu.make_async_copy(context_ref.at[:, part], context_hbm.at[:, part], sems.at[k]))
        sent[-1].start()
    for copy in sent:
        copy.wait()


def finish(base, back, pick, queries, lse, mean):
    rows, wide = queries.shape
    width = base.shape[1] // 2
    inside, outside = pl.BlockSpec(memory_space=pltpu.VMEM), pl.BlockSpec(memory_space=pltpu.HBM)
    return pl.pallas_call(
        finish_kernel,
        name="finish_rows",
        in_specs=[inside] * 6,
        out_specs=[outside] * 3,
        out_shape=(
            jax.ShapeDtypeStruct((rows, width), jnp.bfloat16),
            jax.ShapeDtypeStruct((rows, width), jnp.bfloat16),
            jax.ShapeDtypeStruct((rows, wide), jnp.bfloat16),
        ),
        scratch_shapes=[
            pltpu.VMEM((2, rows, width), jnp.bfloat16),
            pltpu.VMEM((rows, wide), jnp.bfloat16),
            pltpu.SemaphoreType.DMA((width // HEAD_SIZE + 2,)),
        ],
        compiler_params=params(8),
        cost_estimate=cost(4 * rows * wide, 10 * rows * wide),
    )(base, back, pick, queries, lse, mean)


def swap(x, mask, size):
    return lax.ppermute(x, "tp", [(i, i ^ mask) for i in range(size)])


def turn(x, shift, size):
    return lax.ppermute(x, "tp", [(i, (i + shift) % size) for i in range(size)])


def others(x, size):
    return [turn(x, shift, size) for shift in range(1, size)]


def shards(
    hidden_in,
    queries,
    cache_keys,
    cached_value_rows,
    cache_lengths,
    base_key_matrix,
    base_value_matrix,
    shrink_weights,
    pooled_up_weights,
    block_owner,
    block_slot,
):
    rows_here, shard_width = hidden_in.shape
    replicas = lax.axis_size("rep")
    parts = lax.axis_size("tp")
    blocks_here = rows_here // BLK
    capacity = max(2, (2 * blocks_here + replicas - 1) // replicas)

    def all_to_all(x):
        kept = x.shape
        x = x.reshape(replicas, kept[0] // replicas, kept[1])
        return lax.all_to_all(x, "rep", split_axis=0, concat_axis=0, tiled=True).reshape(kept)

    outgoing, pick = pack(block_owner, block_slot, hidden_in, replicas, capacity)
    arrived = all_to_all(outgoing)

    if parts == 4:
        one = swap(hidden_in, 1, parts)
        two = swap(hidden_in, 2, parts)
    mean, lse, shrink_here = cached_attention(cache_lengths, queries, cache_keys, cached_value_rows, shrink_weights)
    arrived, lse = lax.optimization_barrier((arrived, lse))
    partial_rows, sent, flags = shrink(arrived, shrink_here)
    matrices = (base_key_matrix, base_value_matrix)
    if parts == 4:
        pieces = [hidden_in, one]
        received = [swap(sent, mask, parts) for mask in (1, 2, 3)]
    else:
        pieces = [hidden_in] + others(hidden_in, parts)
    early = 1
    sent, *first = lax.optimization_barrier((sent, *pieces[:early]))
    base, up_here = early_products(first, parts, *matrices, pooled_up_weights)
    if parts == 4:
        received[0], base = lax.optimization_barrier((received[0], base))
        sums = [partial_rows] + received
        one, two, _ = lax.optimization_barrier((one, two, received[0]))
        pieces = [hidden_in, one, two, swap(two, 1, parts)]
    else:
        sums = [partial_rows] + others(sent, parts)
    deltas = expand(sums, flags, up_here)
    back = all_to_all(deltas)
    deltas, *between = lax.optimization_barrier((deltas, *pieces[early:-1]))
    base, *last, mean = base_products(between, parts, base, *matrices, mean)
    owner = owner_of(lax.axis_index("tp"), early, parts)
    key_rows = lax.dynamic_slice_in_dim(base_key_matrix, owner * shard_width, shard_width, 0)
    more = jnp.dot(between[0], key_rows, preferred_element_type=jnp.float32)
    base = base + jnp.concatenate([more, jnp.zeros_like(more)], axis=1)
    base = last_product(pieces[-1], *last, base)
    return finish(base, back, pick, queries, lse, mean)


def solution(mesh):
    return jax.shard_map(
        shards,
        mesh=mesh,
        in_specs=(
            P("rep", "tp"),
            P("rep", "tp"),
            P("rep", None, "tp"),
            P("rep", None, "tp"),
            P("rep"),
            P(None, "tp"),
            P(None, "tp"),
            P("rep", "tp", None),
            P("rep", None, None, "tp"),
            P("rep", None),
            P("rep"),
        ),
        out_specs=(P("rep", "tp"), P("rep", "tp"), P("rep", "tp")),
        check_vma=False,
    )
```

```python
import functools

import jax
import jax.numpy as jnp
from jax import lax
from jax.experimental import pallas as pl
from jax.experimental.pallas import tpu as pltpu
from jax.sharding import PartitionSpec as P

HEAD_SIZE = 128
BLK = 4
LANES = 128
MIB = 1 << 20

adapter_scale = 0.5
masked_score = -1e30


def params(mib):
    return pltpu.CompilerParams(vmem_limit_bytes=mib * MIB)


def cost(flops, moved, exps=0):
    return pl.CostEstimate(flops=flops, bytes_accessed=moved, transcendentals=exps)


def pinned(x):
    return pltpu.with_memory_space_constraint(x, pltpu.HBM)


def iota(shape, dim):
    return lax.broadcasted_iota(jnp.int32, shape, dim)


def pack_kernel(capacity, owner_ref, slot_ref, hidden_ref, out_hbm, pick_hbm, out_ref, pick_ref, sems):
    blocks = owner_ref.shape[0]
    rows, width = hidden_ref.shape
    places = out_ref.shape[0]
    square = (blocks, blocks)
    down, across = iota(square, 0), iota(square, 1)
    owner_across = jnp.zeros((1, blocks), jnp.int32)
    owner_down = jnp.zeros((blocks, 1), jnp.int32)
    row_slot = jnp.zeros((rows, 1), jnp.int32)
    for b in range(blocks):
        owner_across = jnp.where(iota((1, blocks), 1) == b, owner_ref[b], owner_across)
        owner_down = jnp.where(iota((blocks, 1), 0) == b, owner_ref[b], owner_down)
        row_slot = jnp.where(iota((rows, 1), 0) // BLK == b, slot_ref[b], row_slot)
    same = (owner_down == owner_across) & (across < down)
    rank = jnp.sum(jnp.where(same, 1.0, 0.0), axis=1, keepdims=True)
    target = owner_down.astype(jnp.float32) * capacity + rank
    spread = iota((blocks, rows), 0) == iota((blocks, rows), 1) // BLK
    row_target = jnp.sum(jnp.where(spread, jnp.broadcast_to(target, (blocks, rows)), 0.0), axis=0, keepdims=True)
    row_target = row_target.astype(jnp.int32) * BLK + iota((1, rows), 1) % BLK
    pick = jnp.where(iota((places, rows), 0) == row_target, 1.0, 0.0).astype(jnp.bfloat16)
    flags = jnp.where(iota((rows, LANES), 1) == row_slot, 1.0, 0.0).astype(jnp.bfloat16)
    sent = []
    part = places // 2
    for n in range(2):
        here = slice(n * part, (n + 1) * part)
        out_ref[here, :width] = jnp.dot(pick[here], hidden_ref[...], preferred_element_type=jnp.float32).astype(jnp.bfloat16)
        out_ref[here, width:] = jnp.dot(pick[here], flags, preferred_element_type=jnp.float32).astype(jnp.bfloat16)
        rows_there = pl.ds(n * part, part)
        sent.append(pltpu.make_async_copy(out_ref.at[rows_there], out_hbm.at[rows_there], sems.at[n]))
        sent[n].start()
    gather = iota((rows, blocks), 1) == iota((rows, blocks), 0) // BLK
    target = jnp.sum(jnp.where(iota(square, 0) == iota(square, 1), target, 0.0), axis=0, keepdims=True)
    target = jnp.sum(jnp.where(gather, target, 0.0), axis=1, keepdims=True)
    target = target.astype(jnp.int32) * BLK + iota((rows, 1), 0) % BLK
    pick_ref[...] = jnp.where(iota((rows, places), 1) == target, 1.0, 0.0).astype(jnp.bfloat16)
    sent.append(pltpu.make_async_copy(pick_ref, pick_hbm, sems.at[2]))
    sent[-1].start()
    for copy in sent:
        copy.wait()


def pack(block_owner, block_slot, hidden, replicas, capacity):
    rows, width = hidden.shape
    places = replicas * capacity * BLK
    scalars = pl.BlockSpec(memory_space=pltpu.SMEM)
    outside = pl.BlockSpec(memory_space=pltpu.HBM)
    return pl.pallas_call(
        functools.partial(pack_kernel, capacity),
        name="pack_rows",
        in_specs=[scalars, scalars, pl.BlockSpec(memory_space=pltpu.VMEM)],
        out_specs=[outside, outside],
        out_shape=(
            pltpu.HBM((places, width + LANES), jnp.bfloat16),
            pltpu.HBM((rows, places), jnp.bfloat16),
        ),
        scratch_shapes=[
            pltpu.VMEM((places, width + LANES), jnp.bfloat16),
            pltpu.VMEM((rows, places), jnp.bfloat16),
            pltpu.SemaphoreType.DMA((3,)),
        ],
        compiler_params=params(61),
        cost_estimate=cost(2 * places * rows * width, 2 * (places + rows) * width),
    )(block_owner[:, 0], block_slot, hidden)


def shrink_kernel(rows_ref, shrink_ref, out_ref, sent_ref, flag_ref):
    pool, width, rank = shrink_ref.shape
    rows = rows_ref[:, :width]
    flag_ref[...] = rows_ref[:, width:]
    total = jnp.zeros(out_ref.shape, jnp.float32)
    for a in range(pool):
        part = jnp.dot(rows, shrink_ref[a], preferred_element_type=jnp.float32)
        total += part * rows_ref[:, width + a : width + a + 1].astype(jnp.float32)
    out_ref[...] = total
    sent_ref[...] = total.astype(jnp.bfloat16)


def shrink(arrived, weights):
    places = arrived.shape[0]
    pool, width, rank = weights.shape
    return pl.pallas_call(
        shrink_kernel,
        name="shrink_rows",
        out_shape=(
            jax.ShapeDtypeStruct((places, rank), jnp.float32),
            jax.ShapeDtypeStruct((places, rank), jnp.bfloat16),
            jax.ShapeDtypeStruct((places, LANES), jnp.bfloat16),
        ),
        compiler_params=params(8),
        cost_estimate=cost(2 * places * width * rank * pool, 2 * (places * width + weights.size)),
    )(arrived, weights)


def expand_kernel(count, *refs):
    parts, flag_ref, up_ref, out_ref = refs[:count], *refs[count:]
    pool, halves, rank, width = up_ref.shape
    total = parts[0][...].astype(jnp.float32)
    for part in parts[1:]:
        total += part[...].astype(jnp.float32)
    shrunk = total.astype(jnp.bfloat16)
    mine = [shrunk * flag_ref[:, a : a + 1] for a in range(pool)]
    side = iota(shrunk.shape, 1) // rank
    wide = [
        jnp.concatenate([jnp.where(side == half, x, jnp.zeros_like(x)) for x in mine], axis=1) for half in range(halves)
    ]
    table = up_ref[...].reshape(pool * halves * rank, width)
    for half in range(halves):
        product = jnp.dot(wide[half], table, preferred_element_type=jnp.float32)
        out_ref[:, half * width : (half + 1) * width] = (adapter_scale * product).astype(jnp.bfloat16)


def expand(parts, flags, up):
    places = parts[0].shape[0]
    pool, halves, rank, width = up.shape
    return pl.pallas_call(
        functools.partial(expand_kernel, len(parts)),
        name="expand_rows",
        out_shape=jax.ShapeDtypeStruct((places, halves * width), jnp.bfloat16),
        compiler_params=params(8),
        cost_estimate=cost(2 * places * up.size, 2 * up.size + 2 * places * halves * width),
    )(*parts, flags, up)


def cached_kernel(heads, group, length_hbm, query_hbm, key_hbm, value_hbm, shrink_hbm, *refs):
    groups = key_hbm.shape[2] // HEAD_SIZE
    mean_hbm, lse_ref, shrink_ref, length_ref, query_ref, keys, values, mean_ref, wide_q, wide_o, sems, more = refs
    rows, window, width = keys.shape
    each = heads // groups
    packed = LANES // heads
    inverse_root = HEAD_SIZE ** (-0.5)

    def copies(i):
        here = pl.ds(i * group, group)
        return (
            pltpu.make_async_copy(key_hbm.at[here], keys.at[here], sems.at[0, i]),
            pltpu.make_async_copy(value_hbm.at[here], values.at[here], sems.at[1, i]),
        )

    ahead = 2
    for i in range(ahead):
        for copy in copies(i):
            copy.start()
    small = [(length_hbm, length_ref), (query_hbm, query_ref), (shrink_hbm, shrink_ref)]
    small = [pltpu.make_async_copy(a, b, more.at[n]) for n, (a, b) in enumerate(small)]
    for copy in small:
        copy.start()
    wide_q[...] = jnp.zeros_like(wide_q)
    lane = iota((window, LANES), 1) // heads
    position = iota((window, LANES), 0)
    sublane = iota((packed, LANES), 0)

    small[0].wait()
    small[1].wait()

    def finished(i):
        here = pl.ds(pl.multiple_of(i * group, group), group)
        return pltpu.make_async_copy(mean_ref.at[here], mean_hbm.at[here], sems.at[2, i])

    def step(i, carry):
        start = pl.multiple_of(i * group, group)
        for h in range(heads):
            part = query_ref[pl.ds(start, group), h * HEAD_SIZE : (h + 1) * HEAD_SIZE]
            wide_q[h // each, pl.ds(h, group, stride=heads), :] = part.astype(jnp.float32)
        key_copy, value_copy = copies(i)
        key_copy.wait()

        @pl.when(i + ahead < rows // group)
        def _():
            for copy in copies(i + ahead):
                copy.start()

        all_weights = []
        for first in range(0, group, packed):
            here = pl.ds(first * heads, LANES)
            query = jnp.concatenate([wide_q[k, here, :] for k in range(groups)], axis=1).astype(jnp.bfloat16)
            block = keys[pl.ds(start + first, packed)].reshape(packed * window, width)
            product = lax.dot_general(block, query, (((1,), (1,)), ((), ())), preferred_element_type=jnp.float32)
            scores = jnp.zeros((window, LANES), jnp.float32)
            limit = jnp.zeros((1, LANES), jnp.int32)
            for r in range(packed):
                scores = jnp.where(lane == r, product[r * window : (r + 1) * window], scores)
                limit = jnp.where(lane[:1] == r, length_ref[start + first + r], limit)
            scores = jnp.where(position < limit, scores * inverse_root, masked_score)
            highest = jnp.max(scores, axis=0, keepdims=True)
            terms = jnp.exp(scores - highest)
            total = jnp.sum(terms, axis=0, keepdims=True)
            all_weights.append(jnp.transpose(terms * (1.0 / total)).astype(jnp.bfloat16))
            logs = jnp.broadcast_to(highest + jnp.log(total), (packed, LANES))
            spread = logs
            for r in range(1, packed):
                spread = jnp.where(sublane == r, pltpu.roll(logs, LANES - r * heads, 1), spread)
            lse_ref[pl.ds(start + first, packed), :] = spread
        value_copy.wait()
        for r in range(0, group, 2):
            weights = all_weights[r // packed][(r % packed) * heads : (r % packed + 2) * heads]
            upper = iota(weights.shape, 0) < heads
            zero = jnp.zeros_like(weights)
            weights = jnp.concatenate([jnp.where(upper, weights, zero), jnp.where(upper, zero, weights)], axis=1)
            block = values[pl.ds(start + r, 2)].reshape(2 * window, width)
            mixed = jnp.dot(weights, block, preferred_element_type=jnp.float32)
            for j in range(2):
                for k in range(groups):
                    mine = pl.ds((r + j) * heads + k * each, each)
                    top = j * heads + k * each
                    wide_o[mine, :] = mixed[top : top + each, k * HEAD_SIZE : (k + 1) * HEAD_SIZE]
        for h in range(heads):
            mean_ref[pl.ds(start, group), h * HEAD_SIZE : (h + 1) * HEAD_SIZE] = wide_o[pl.ds(h, group, stride=heads), :]
        finished(i).start()
        return carry

    lax.fori_loop(0, rows // group, step, 0)
    for i in range(rows // group):
        finished(i).wait()
    small[2].wait()


def cached_attention(lengths, queries, keys, values, weights):
    rows, window, width = keys.shape
    wide = queries.shape[1]
    heads = wide // HEAD_SIZE
    group = max(16, LANES // heads)
    groups = width // HEAD_SIZE
    inside, outside = pl.BlockSpec(memory_space=pltpu.VMEM), pl.BlockSpec(memory_space=pltpu.HBM)
    return pl.pallas_call(
        functools.partial(cached_kernel, heads, group),
        name="cached_attention",
        in_specs=[outside] * 5,
        out_specs=[outside, inside, inside],
        scratch_shapes=[
            pltpu.SMEM(lengths.shape, lengths.dtype),
            pltpu.VMEM(queries.shape, queries.dtype),
            pltpu.VMEM(keys.shape, keys.dtype),
            pltpu.VMEM(values.shape, values.dtype),
            pltpu.VMEM((rows, wide), jnp.float32),
            pltpu.VMEM((groups, group * heads, HEAD_SIZE), jnp.float32),
            pltpu.VMEM((group * heads, HEAD_SIZE), jnp.float32),
            pltpu.SemaphoreType.DMA((3, rows // group)),
            pltpu.SemaphoreType.DMA((3,)),
        ],
        out_shape=[
            pltpu.HBM((rows, wide), jnp.float32),
            jax.ShapeDtypeStruct((rows, LANES), jnp.float32),
            jax.ShapeDtypeStruct(weights.shape, weights.dtype),
        ],
        compiler_params=params(20),
        cost_estimate=cost(4 * rows * heads * window * width, 4 * keys.size + 6 * rows * wide, rows * heads * window),
    )(*(pinned(x) for x in (lengths, queries, keys, values, weights)))


def owner_of(p, parts):
    place = lax.axis_index("tp")
    if parts != 4:
        return lax.rem(place + parts - p, parts)
    if p in (0, 3):
        return place ^ p
    odd = lax.rem(lax.axis_index("rep"), 2)
    return place ^ (p + odd if p == 1 else p - odd)


def early_kernel(count, total, *refs):
    pieces, (key_hbm, value_hbm, up_hbm, out_ref, up_ref, keys, values, sems) = refs[:count], refs[count:]
    shard, width = keys.shape[1:]
    copies = []
    for p in range(count):
        rows = pl.ds(pl.multiple_of(owner_of(p, total) * shard, shard), shard)
        copies.append(pltpu.make_async_copy(key_hbm.at[rows], keys.at[p], sems.at[0, p]))
        copies.append(pltpu.make_async_copy(value_hbm.at[rows], values.at[p], sems.at[1, p]))
    copies.append(pltpu.make_async_copy(up_hbm, up_ref, sems.at[0, count]))
    for copy in copies:
        copy.start()
    for p in range(count):
        for half, weights in enumerate((keys, values)):
            here = slice(half * width, (half + 1) * width)
            copies[2 * p + half].wait()
            product = jnp.dot(pieces[p][...], weights[p], preferred_element_type=jnp.float32)
            out_ref[:, here] = out_ref[:, here] + product if p else product
    copies[-1].wait()


def early_products(pieces, total, key_matrix, value_matrix, up):
    rows, shard = pieces[0].shape
    width = key_matrix.shape[1]
    count = len(pieces)
    inside, outside = pl.BlockSpec(memory_space=pltpu.VMEM), pl.BlockSpec(memory_space=pltpu.HBM)
    return pl.pallas_call(
        functools.partial(early_kernel, count, total),
        name="early_products",
        in_specs=[inside] * count + [outside, outside, outside],
        out_specs=[inside, inside],
        out_shape=[jax.ShapeDtypeStruct((rows, 2 * width), jnp.float32), jax.ShapeDtypeStruct(up.shape, up.dtype)],
        scratch_shapes=[pltpu.VMEM((count, shard, width), key_matrix.dtype)] * 2
        + [pltpu.SemaphoreType.DMA((2, count + 1))],
        compiler_params=params(12),
        cost_estimate=cost(4 * count * rows * shard * width, 4 * count * shard * width),
    )(*pieces, pinned(key_matrix), pinned(value_matrix), pinned(up))


def base_kernel(first, total, *refs):
    count = total - 1 - first
    pieces, refs = refs[:count], refs[count:]
    so_far, key_hbm, value_hbm, mean_hbm, out_ref, last_keys, last_values, mean_ref, keys, values, sems = refs
    shard, width = last_keys.shape

    def copies(p):
        rows = pl.ds(pl.multiple_of(owner_of(p + first, total) * shard, shard), shard)
        key_to, value_to = (last_keys, last_values) if p == count else (keys.at[p], values.at[p])
        key_copy = pltpu.make_async_copy(key_hbm.at[rows], key_to, sems.at[0, p]) if p > 0 else None
        return key_copy, pltpu.make_async_copy(value_hbm.at[rows], value_to, sems.at[1, p])

    everything = [copy for p in range(count + 1) for copy in copies(p) if copy is not None]
    everything.append(pltpu.make_async_copy(mean_hbm, mean_ref, sems.at[0, 0]))
    for copy in everything:
        copy.start()
    out_ref[...] = so_far[...]
    for p in range(count):
        for half, (copy, weights) in enumerate(zip(copies(p), (keys, values))):
            if copy is None:
                continue
            here = slice(half * width, (half + 1) * width)
            copy.wait()
            out_ref[:, here] += jnp.dot(pieces[p][...], weights[p], preferred_element_type=jnp.float32)
    for copy in everything[-3:]:
        copy.wait()


def base_products(pieces, total, so_far, key_matrix, value_matrix, mean):
    rows, shard = pieces[0].shape
    width = key_matrix.shape[1]
    count = len(pieces)
    inside, outside = pl.BlockSpec(memory_space=pltpu.VMEM), pl.BlockSpec(memory_space=pltpu.HBM)
    last = jax.ShapeDtypeStruct((shard, width), key_matrix.dtype)
    return pl.pallas_call(
        functools.partial(base_kernel, total - 1 - count, total),
        name="base_products",
        in_specs=[inside] * (count + 1) + [outside] * 3,
        out_specs=[inside] * 4,
        scratch_shapes=[
            pltpu.VMEM((count, shard, width), key_matrix.dtype),
            pltpu.VMEM((count, shard, width), key_matrix.dtype),
            pltpu.SemaphoreType.DMA((2, count + 1)),
        ],
        out_shape=[
            jax.ShapeDtypeStruct((rows, 2 * width), jnp.float32),
            last,
            last,
            jax.ShapeDtypeStruct(mean.shape, mean.dtype),
        ],
        compiler_params=params(16),
        cost_estimate=cost(4 * count * rows * shard * width, count * (4 * shard * width + 2 * rows * shard)),
    )(*pieces, so_far, pinned(key_matrix), pinned(value_matrix), pinned(mean))


def last_kernel(piece_ref, keys, values, base_ref, out_ref):
    width = keys.shape[1]
    for half, weights in enumerate((keys, values)):
        here = slice(half * width, (half + 1) * width)
        product = jnp.dot(piece_ref[...], weights[...], preferred_element_type=jnp.float32)
        out_ref[:, here] = base_ref[:, here] + product


def last_product(late, keys, values, base):
    return pl.pallas_call(
        last_kernel,
        name="last_product",
        out_shape=jax.ShapeDtypeStruct(base.shape, base.dtype),
        compiler_params=params(8),
        cost_estimate=cost(2 * late.size * base.shape[1], 4 * keys.size),
    )(late, keys, values, base)


def finish_kernel(base_ref, back_ref, pick_ref, query_ref, lse_ref, mean_ref, *refs):
    new_key_hbm, new_value_hbm, context_hbm, new_ref, context_ref, sems = refs
    rows, wide = query_ref.shape
    width = new_ref.shape[2]
    heads = wide // HEAD_SIZE
    groups = width // HEAD_SIZE
    each = heads // groups
    inverse_root = HEAD_SIZE ** (-0.5)
    delta = jnp.dot(pick_ref[...], back_ref[...], preferred_element_type=jnp.float32)
    base = (base_ref[...] + delta).astype(jnp.bfloat16)
    sent = []
    for half, target in enumerate((new_key_hbm, new_value_hbm)):
        new_ref[half] = base[:, half * width : (half + 1) * width]
        sent.append(pltpu.make_async_copy(new_ref.at[half], target, sems.at[groups + half]))
        sent[half].start()
    keys, values = base[:, :width].astype(jnp.float32), base[:, width:].astype(jnp.float32)
    column = iota((rows, LANES), 1)
    own = jnp.zeros((rows, LANES), jnp.float32)
    for h in range(heads):
        k = h // each
        query = query_ref[:, h * HEAD_SIZE : (h + 1) * HEAD_SIZE].astype(jnp.float32)
        score = jnp.sum(query * keys[:, k * HEAD_SIZE : (k + 1) * HEAD_SIZE], axis=1, keepdims=True)
        own = jnp.where(column == h, score * inverse_root, own)
    share = 1.0 / (1.0 + jnp.exp(lse_ref[...] - own))
    for k in range(groups):
        for h in range(k * each, (k + 1) * each):
            mean = mean_ref[:, h * HEAD_SIZE : (h + 1) * HEAD_SIZE]
            mixed = mean + share[:, h : h + 1] * (values[:, k * HEAD_SIZE : (k + 1) * HEAD_SIZE] - mean)
            context_ref[:, h * HEAD_SIZE : (h + 1) * HEAD_SIZE] = mixed.astype(jnp.bfloat16)
        part = pl.ds(k * each * HEAD_SIZE, each * HEAD_SIZE)
        sent.append(pltpu.make_async_copy(context_ref.at[:, part], context_hbm.at[:, part], sems.at[k]))
        sent[-1].start()
    for copy in sent:
        copy.wait()


def finish(base, back, pick, queries, lse, mean):
    rows, wide = queries.shape
    width = base.shape[1] // 2
    inside, outside = pl.BlockSpec(memory_space=pltpu.VMEM), pl.BlockSpec(memory_space=pltpu.HBM)
    return pl.pallas_call(
        finish_kernel,
        name="finish_rows",
        in_specs=[inside] * 6,
        out_specs=[outside] * 3,
        out_shape=(
            jax.ShapeDtypeStruct((rows, width), jnp.bfloat16),
            jax.ShapeDtypeStruct((rows, width), jnp.bfloat16),
            jax.ShapeDtypeStruct((rows, wide), jnp.bfloat16),
        ),
        scratch_shapes=[
            pltpu.VMEM((2, rows, width), jnp.bfloat16),
            pltpu.VMEM((rows, wide), jnp.bfloat16),
            pltpu.SemaphoreType.DMA((width // HEAD_SIZE + 2,)),
        ],
        compiler_params=params(8),
        cost_estimate=cost(4 * rows * wide, 10 * rows * wide),
    )(base, back, pick, queries, lse, mean)


def swap(x, mask, size):
    return lax.ppermute(x, "tp", [(i, i ^ mask) for i in range(size)])


def cross(x, masks, size):
    pairs = [(r * size + i, r * size + (i ^ masks[r % 2])) for r in range(lax.axis_size("rep")) for i in range(size)]
    return lax.ppermute(x, ("rep", "tp"), pairs)


def turn(x, shift, size):
    return lax.ppermute(x, "tp", [(i, (i + shift) % size) for i in range(size)])


def others(x, size):
    return [turn(x, shift, size) for shift in range(1, size)]


def shards(
    hidden_in,
    queries,
    cache_keys,
    cached_value_rows,
    cache_lengths,
    base_key_matrix,
    base_value_matrix,
    shrink_weights,
    pooled_up_weights,
    block_owner,
    block_slot,
):
    rows_here, shard_width = hidden_in.shape
    replicas = lax.axis_size("rep")
    parts = lax.axis_size("tp")
    blocks_here = rows_here // BLK
    capacity = max(2, (2 * blocks_here + replicas - 1) // replicas)

    def all_to_all(x):
        kept = x.shape
        x = x.reshape(replicas, kept[0] // replicas, kept[1])
        return lax.all_to_all(x, "rep", split_axis=0, concat_axis=0, tiled=True).reshape(kept)

    outgoing, pick = pack(block_owner, block_slot, hidden_in, replicas, capacity)
    arrived = all_to_all(outgoing)

    if parts == 4:
        one = cross(hidden_in, (1, 2), parts)
        two = cross(hidden_in, (2, 1), parts)
    mean, lse, shrink_here = cached_attention(cache_lengths, queries, cache_keys, cached_value_rows, shrink_weights)
    arrived, lse = lax.optimization_barrier((arrived, lse))
    partial_rows, sent, flags = shrink(arrived, shrink_here)
    matrices = (base_key_matrix, base_value_matrix)
    if parts == 4:
        pieces = [hidden_in, one]
        received = [swap(sent, mask, parts) for mask in (1, 2, 3)]
    else:
        pieces = [hidden_in] + others(hidden_in, parts)
    early = 1
    sent, *first = lax.optimization_barrier((sent, *pieces[:early]))
    base, up_here = early_products(first, parts, *matrices, pooled_up_weights)
    if parts == 4:
        received[0], base = lax.optimization_barrier((received[0], base))
        sums = [partial_rows] + received
        one, two, _ = lax.optimization_barrier((one, two, received[0]))
        far = jnp.where(lax.rem(lax.axis_index("rep"), 2) == 1, one, two)
        far, sums[0] = lax.optimization_barrier((far, partial_rows))
        pieces = [hidden_in, one, two, swap(far, 1, parts)]
    else:
        sums = [partial_rows] + others(sent, parts)
    deltas = expand(sums, flags, up_here)
    back = all_to_all(deltas)
    deltas, *between = lax.optimization_barrier((deltas, *pieces[early:-1]))
    base, *last, mean = base_products(between, parts, base, *matrices, mean)
    owner = owner_of(early, parts)
    key_rows = lax.dynamic_slice_in_dim(base_key_matrix, owner * shard_width, shard_width, 0)
    more = jnp.dot(between[0], key_rows, preferred_element_type=jnp.float32)
    base = base + jnp.concatenate([more, jnp.zeros_like(more)], axis=1)
    base = last_product(pieces[-1], *last, base)
    return finish(base, back, pick, queries, lse, mean)


def solution(mesh):
    return jax.shard_map(
        shards,
        mesh=mesh,
        in_specs=(
            P("rep", "tp"),
            P("rep", "tp"),
            P("rep", None, "tp"),
            P("rep", None, "tp"),
            P("rep"),
            P(None, "tp"),
            P(None, "tp"),
            P("rep", "tp", None),
            P("rep", None, None, "tp"),
            P("rep", None),
            P("rep"),
        ),
        out_specs=(P("rep", "tp"), P("rep", "tp"), P("rep", "tp")),
        check_vma=False,
    )
```
